256 devices in a mesh: section: 4 (over x), ctx: 64 (over y, z, core).
Axes of the slice: x: 4, y: 4, z: 8, core: 2. Of those that a mesh axis runs over, the one named last changes fastest.
Arguments:
- queries: bfloat16 [32768, 4096], P(('section', 'ctx')), may hold values from -40 to 40
- keys: bfloat16 [32768, 512], P(('section', 'ctx')), may hold values from -6 to 6
- values: bfloat16 [32768, 512], P(('section', 'ctx')), may hold values from -6 to 6
- keep_index: int32 [256, 4, 8], P(('section', 'ctx')), may hold values from 0 to 127, as said below
Outputs:
- attended: bfloat16 [32768, 4096], P(('section', 'ctx'))
The draws below stay inside these ranges and needn't reach their ends.
Inputs may be any that keep to these rules, and one draw needn't show every extreme that they name: `keep_index`: for each block and key and value head, 8 distinct positions in increasing order.
All inputs are finite; a program needn't handle non-finite values.
Results may differ from the reference program's by a relative error of at most 0.0085.
Values may be sent and summed in bfloat16 or wider, within the bound.
No kernel may reach another device: no remote copies, remote signals or barrier semaphores. Data moves between devices by JAX's collectives and lax.ppermute only.
A program may use at most 128 MiB of HBM per device.

```python
import math
import jax
import jax.numpy as jnp
from jax import lax

QH = 32
KVH = 4
HD = 128
KEEP = 8
TOK_DEV = 128
TOKENS = 32768


def draw_keys(key, part):
    own_key = jax.random.fold_in(key, 11)
    result = jnp.clip(jax.random.normal(own_key, (TOKENS, KVH * HD), jnp.float32), -6.0, 6.0)
    return result.astype(jnp.bfloat16)


def draw_queries(key, part):
    own_key = jax.random.fold_in(key, 12)
    result = jnp.clip(jax.random.normal(own_key, (TOKENS, QH * HD), jnp.float32), -6.0, 6.0)
    return result.astype(jnp.bfloat16)


def draw_keep_index(key, part):
    key = jax.random.fold_in(key, 13)
    block_count = TOKENS // TOK_DEV
    subkeys = jax.random.split(key, block_count * KVH)

    def pick_rows(subkey):
        return jnp.sort(jax.random.permutation(subkey, TOK_DEV)[:KEEP])
    picked = jax.vmap(pick_rows)(subkeys)
    return picked.reshape(block_count, KVH, KEEP).astype(jnp.int32)


def steps_of(key, shape, cuts, least, top_value):
    gain = 1.0
    for dim, parts in cuts:
        heights = jax.random.uniform(jax.random.fold_in(jax.random.fold_in(key, 6), dim), (parts,), jnp.float32, least / len(cuts), top_value / len(cuts))
        gain = gain * jnp.repeat(jnp.exp(heights), shape[dim] // parts).reshape((-1,) + (1,) * (len(shape) - 1 - dim))
    return gain


def centred(key, dims, deviation, reach, shards=(), kind=jnp.bfloat16):
    entries = deviation * jax.random.normal(key, dims, jnp.float32)
    if shards:
        entries = entries * steps_of(key, dims, shards, -0.22, 0.18)
    return jnp.clip(entries, -reach, reach).astype(kind)


def setup_inputs(seed: int = 0) -> dict:
    streams_of = jax.random.split(jax.random.key(seed), 5)
    queries = draw_queries(jax.random.fold_in(streams_of[4], 71), 0)
    keys = draw_keys(jax.random.fold_in(streams_of[4], 71), 0)
    values = centred(streams_of[2], (TOKENS, KVH * HD), 1.0, 6.0, ((0, 256),))
    keep_index = draw_keep_index(jax.random.fold_in(streams_of[4], 71), 0)
    return {"queries": queries, "keys": keys, "values": values, "keep_index": keep_index}


def reference(queries, keys, values, keep_index):
    block_count = TOKENS // TOK_DEV
    group_size = QH // KVH
    score_scale = 1.0 / math.sqrt(HD)
    query_blocks = queries.reshape(block_count, TOK_DEV, KVH, group_size, HD)
    key_blocks = keys.reshape(block_count, TOK_DEV, KVH, HD)
    value_blocks = values.reshape(block_count, TOK_DEV, KVH, HD)
    chosen = keep_index[..., None]
    kept_keys = jnp.take_along_axis(jnp.transpose(key_blocks, (0, 2, 1, 3)), chosen, axis=2)
    kept_values = jnp.take_along_axis(jnp.transpose(value_blocks, (0, 2, 1, 3)), chosen, axis=2)
    flat_keys = jnp.transpose(kept_keys, (0, 2, 1, 3)).reshape(block_count * KEEP, KVH, HD)
    flat_values = jnp.transpose(kept_values, (0, 2, 1, 3)).reshape(block_count * KEEP, KVH, HD)
    kept_owner = (jnp.arange(block_count * KEEP) // KEEP).astype(jnp.int32)
    position = jnp.arange(TOK_DEV)
    causal = position[None, :] <= position[:, None]

    def per_host(operands):
        query_rows, key_rows, value_rows, host = operands
        all_keys = jnp.concatenate([key_blocks[0], flat_keys, key_rows], axis=0).astype(jnp.float32)
        all_values = jnp.concatenate([value_blocks[0], flat_values, value_rows], axis=0).astype(jnp.float32)
        scores = jnp.einsum('tkgd,skd->tkgs', query_rows.astype(jnp.float32), all_keys) * score_scale
        anchor_ok = jnp.broadcast_to(host > 0, (TOK_DEV, TOK_DEV))
        kept_ok = jnp.broadcast_to((kept_owner >= 1) & (kept_owner < host), (TOK_DEV, block_count * KEEP))
        allowed = jnp.concatenate([anchor_ok, kept_ok, causal], axis=1)[:, None, None, :]
        masked = jnp.where(allowed, scores, -1e+30)
        highest = lax.optimization_barrier(jnp.max(masked, axis=-1, keepdims=True))
        weights = jnp.where(allowed, jnp.exp(masked - highest), 0.0)
        total = lax.optimization_barrier(jnp.sum(weights, axis=-1))
        rounded = weights.astype(jnp.bfloat16).astype(jnp.float32)
        summed = jnp.einsum('tkgs,skd->tkgd', rounded, all_values)
        result = summed / total[..., None]
        return result.reshape(TOK_DEV, QH * HD).astype(jnp.bfloat16)
    hosts = jnp.arange(block_count, dtype=jnp.int32)
    outputs = lax.map(per_host, (query_blocks, key_blocks, value_blocks, hosts))
    return outputs.reshape(TOKENS, QH * HD)
```

```python
import functools
import math

import jax
import jax.numpy as jnp
from jax import lax
from jax.experimental import pallas as pl
from jax.experimental.pallas import tpu as pltpu
from jax.sharding import Mesh, PartitionSpec as P

QH = 32
KVH = 4
HD = 128
KEEP = 8
TOK = 128
GROUP = QH // KVH
NX, NY, NZ, NC = 4, 4, 8, 2
NXY = NX * NY
HALF = KVH // NC
AXES = ("x", "y", "z", "c")
PIECE = HALF * 2 * TOK // NXY
FAR = NXY * NZ * NC * KEEP
SLOT = HALF * 2 * TOK + PIECE
EXP2_SCALE = math.log2(math.e) / math.sqrt(HD)
VMEM_BYTES = 48 * 1024 * 1024

bf16 = jnp.bfloat16
f32 = jnp.float32


def pick_kernel(index_ref, keys_ref, values_ref, kept_ref, block_ref):
    rows = lax.broadcasted_iota(jnp.int32, (KEEP, TOK), 0)
    lanes = lax.broadcasted_iota(jnp.int32, (KEEP, TOK), 1)
    for j in range(KVH):
        chosen = jnp.zeros((KEEP, TOK), jnp.int32)
        for r in range(KEEP):
            chosen = jnp.where(rows == r, index_ref[0, j, r], chosen)
        onehot = (chosen == lanes).astype(f32).astype(bf16)
        columns = slice(j * HD, (j + 1) * HD)
        key_rows = jnp.dot(onehot, keys_ref[:, columns], preferred_element_type=f32)
        value_rows = jnp.dot(onehot, values_ref[:, columns], preferred_element_type=f32)
        kept_ref[j] = jnp.concatenate([key_rows, value_rows], axis=0).astype(bf16)
        block_ref[j, :TOK] = keys_ref[:, columns]
        block_ref[j, TOK:] = values_ref[:, columns]


def pick(keep_index, keys, values):
    return pl.pallas_call(
        pick_kernel,
        in_specs=[
            pl.BlockSpec(memory_space=pltpu.SMEM),
            pl.BlockSpec(memory_space=pltpu.VMEM),
            pl.BlockSpec(memory_space=pltpu.VMEM),
        ],
        out_shape=(
            jax.ShapeDtypeStruct((KVH, 2 * KEEP, HD), bf16),
            jax.ShapeDtypeStruct((KVH, 2 * TOK, HD), bf16),
        ),
    )(keep_index, keys, values)


def pair_kernel(core_ref, mine_ref, other_ref, pair_ref):
    first = core_ref[0] == 0
    for h in range(HALF):
        mine = mine_ref[h].astype(f32)
        other = other_ref[h].astype(f32)
        low = jnp.where(first, mine, other)
        high = jnp.where(first, other, mine)
        pair_ref[h, 0] = jnp.concatenate([low[:KEEP], high[:KEEP]], axis=0).astype(bf16)
        pair_ref[h, 1] = jnp.concatenate([low[KEEP:], high[KEEP:]], axis=0).astype(bf16)


def attend_kernel(place_ref, q_ref, k_ref, v_ref, far_ref, _, out_ref, key_rows, value_rows):
    block = place_ref[1]
    head = pl.program_id(0)
    first_key = k_ref[0:1, :].astype(f32)
    own_at, anchor_at = FAR + TOK, FAR
    lane_ones = jnp.ones((TOK, HD), f32)

    def put(at, keys, values, valid):
        keys = jnp.where(valid, keys.astype(f32), first_key)
        values = jnp.where(valid, values.astype(f32), 0.0)
        key_rows[pl.ds(at, TOK), :] = keys.astype(bf16)
        value_rows[pl.ds(at, TOK), :HD] = values.astype(bf16)
        value_rows[pl.ds(at, TOK), HD:] = jnp.where(valid, lane_ones, 0.0).astype(bf16)

    row_block = lax.broadcasted_iota(jnp.int32, (TOK, HD), 0) // KEEP

    at_head = pl.multiple_of(head * 2 * TOK, 2 * TOK)
    for s in range(NXY):
        owner = row_block + s * (TOK // KEEP)
        put(
            s * TOK,
            far_ref[s, pl.ds(at_head, TOK), :],
            far_ref[s, pl.ds(at_head + TOK, TOK), :],
            (owner >= 1) & (owner < block),
        )
    pieces = TOK // PIECE
    anchor_keys = [far_ref[head * 2 * pieces + i, HALF * 2 * TOK :, :] for i in range(pieces)]
    anchor_values = [
        far_ref[head * 2 * pieces + pieces + i, HALF * 2 * TOK :, :] for i in range(pieces)
    ]
    put(
        anchor_at,
        jnp.concatenate(anchor_keys, axis=0),
        jnp.concatenate(anchor_values, axis=0),
        row_block * 0 < block,
    )
    key_rows[own_at:, :] = k_ref[...]
    value_rows[own_at:, :HD] = v_ref[...]
    value_rows[own_at:, HD:] = lane_ones.astype(bf16)

    causal = lax.broadcasted_iota(jnp.int32, (TOK, TOK), 1) <= lax.broadcasted_iota(
        jnp.int32, (TOK, TOK), 0
    )
    for g in range(GROUP):
        columns = slice(g * HD, (g + 1) * HD)
        scores = lax.dot_general(
            q_ref[:, columns], key_rows[...], (((1,), (1,)), ((), ())), preferred_element_type=f32
        )
        scores = jnp.concatenate(
            [scores[:, :own_at], jnp.where(causal, scores[:, own_at:], -1e30)], axis=1
        )
        highest = jnp.max(scores, axis=1, keepdims=True)
        weights = jnp.exp2((scores - highest) * EXP2_SCALE).astype(bf16)
        summed = jnp.dot(weights, value_rows[...], preferred_element_type=f32)
        out_ref[:, columns] = (summed[:, :HD] / summed[:, HD:]).astype(bf16)


def attend(place, queries, keys, values, far, out, first):
    def heads(i, place_ref):
        return (0, place_ref[0 if first else 2] * HALF + i)

    whole = pl.BlockSpec((NXY, SLOT, HD), lambda i, place_ref: (0, 0, 0))
    grid_spec = pltpu.PrefetchScalarGridSpec(
        num_scalar_prefetch=1,
        grid=(HALF,),
        in_specs=[
            pl.BlockSpec((TOK, GROUP * HD), heads),
            pl.BlockSpec((TOK, HD), heads),
            pl.BlockSpec((TOK, HD), heads),
            whole,
            pl.BlockSpec(memory_space=pl.ANY),
        ],
        out_specs=pl.BlockSpec((TOK, GROUP * HD), heads),
        scratch_shapes=[
            pltpu.VMEM((FAR + 2 * TOK, HD), bf16),
            pltpu.VMEM((FAR + 2 * TOK, 2 * HD), bf16),
        ],
    )
    return pl.pallas_call(
        attend_kernel,
        grid_spec=grid_spec,
        out_shape=jax.ShapeDtypeStruct((TOK, QH * HD), bf16),
        input_output_aliases={5: 0},
        compiler_params=pltpu.CompilerParams(vmem_limit_bytes=VMEM_BYTES),
        cost_estimate=pl.CostEstimate(
            flops=2 * 2 * HALF * GROUP * TOK * (FAR + 2 * TOK) * HD,
            bytes_accessed=4 * 1024 * 1024,
            transcendentals=HALF * GROUP * TOK * (FAR + 2 * TOK),
        ),
    )(place, queries, keys, values, far, out)


def on_device(queries, keys, values, keep_index):
    core = lax.axis_index("c")
    xy = lax.axis_index("x") * NY + lax.axis_index("y")
    block = (xy * NZ + lax.axis_index("z")) * NC + core
    place = jnp.stack([core, block, 1 - core]).astype(jnp.int32)
    swap = [(0, 1), (1, 0)]
    to_all = functools.partial(lax.all_to_all, split_axis=0, concat_axis=0, tiled=True)

    kept, own = pick(keep_index, keys, values)
    half = lambda a, which: lax.dynamic_slice_in_dim(a, which * HALF, HALF, 0)
    sent = jnp.concatenate([half(kept, 1 - core), half(own, 1 - core)], axis=1)
    came = lax.ppermute(sent, "c", swap)
    pair = pl.pallas_call(
        pair_kernel,
        in_specs=[
            pl.BlockSpec(memory_space=pltpu.SMEM),
            pl.BlockSpec(memory_space=pltpu.VMEM),
            pl.BlockSpec(memory_space=pltpu.VMEM),
        ],
        out_shape=jax.ShapeDtypeStruct((HALF, 2, 2 * KEEP, HD), bf16),
    )(place, half(kept, core), came[:, : 2 * KEEP])

    anchor = jnp.where(core == 0, half(own, core), came[:, 2 * KEEP :])
    piece = to_all(anchor.reshape(NXY * PIECE, HD), ("x", "y"))[:PIECE]

    rows = HALF * 2 * 2 * KEEP
    along_z = to_all(
        jnp.tile(jnp.concatenate([pair.reshape(rows, HD), piece], axis=0)[None], (NZ, 1, 1)), "z"
    )
    retained = along_z[:, :rows].reshape(NZ, HALF, 2, 2 * KEEP, HD)
    retained = jnp.transpose(retained, (1, 2, 0, 3, 4)).reshape(HALF * 2 * TOK, HD)
    slot = jnp.concatenate([retained, along_z[0, rows:]], axis=0)
    far = to_all(jnp.tile(slot[None], (NXY, 1, 1)), ("x", "y"))
    far_other = lax.ppermute(far, "c", swap)

    out = jnp.zeros((TOK, QH * HD), bf16)
    out = attend(place, queries, keys, values, far, out, True)
    return attend(place, queries, keys, values, far_other, out, False)


def solution(mesh):
    fine = Mesh(mesh.devices.reshape(NX, NY, NZ, NC), AXES)
    return jax.shard_map(
        on_device,
        mesh=fine,
        in_specs=(P(AXES, None), P(AXES, None), P(AXES, None), P(AXES, None, None)),
        out_specs=P(AXES, None),
        check_vma=False,
    )
```

```python
import functools
import math

import jax
import jax.numpy as jnp
from jax import lax
from jax.experimental import pallas as pl
from jax.experimental.pallas import tpu as pltpu
from jax.sharding import Mesh, PartitionSpec as P

QH = 32
KVH = 4
HD = 128
KEEP = 8
TOK = 128
GROUP = QH // KVH
NX, NY, NZ, NC = 4, 4, 8, 2
DEVICES = NX * NY * NZ * NC
HALF = KVH // NC
FIRST = 16
SECOND = 8
PAIR = NC * KEEP
KEPT_ROWS = HALF * 2 * PAIR
PIECE = HALF * 2 * TOK // FIRST
CHUNK = FIRST * PAIR
FAR = SECOND * CHUNK
SLOT = HALF * 2 * CHUNK + PIECE
EXP2_SCALE = math.log2(math.e) / math.sqrt(HD)
VMEM_BYTES = 48 * 1024 * 1024

bf16 = jnp.bfloat16
f32 = jnp.float32
in_smem = pl.BlockSpec(memory_space=pltpu.SMEM)
in_vmem = pl.BlockSpec(memory_space=pltpu.VMEM)


def device(core, a, u, zh, zl):
    x, y = (a, u) if core == 0 else (u, a)
    z = (2 * zh + zl) % NZ if core == 0 else (2 * zh - zl) % NZ
    return ((x * NY + y) * NZ + z) * NC + core


def first_groups():
    return [
        [device(c, a, u, zh, zl) for u in range(4) for zh in range(4)]
        for c in range(2)
        for a in range(4)
        for zl in range(2)
    ]


def second_groups():
    return [
        [device(c, a, u, zh, zl) for a in range(4) for zl in range(2)]
        for c in range(2)
        for u in range(4)
        for zh in range(4)
    ]


def pick_kernel(block_ref, index_ref, keys_ref, values_ref, mine_ref, sent_ref):
    core = block_ref[0] % NC
    rows = lax.broadcasted_iota(jnp.int32, (KEEP, TOK), 0)
    lanes = lax.broadcasted_iota(jnp.int32, (KEEP, TOK), 1)
    for out_ref, owner in ((sent_ref, 1 - core), (mine_ref, core)):
        for h in range(HALF):
            j = owner * HALF + h
            chosen = jnp.zeros((KEEP, TOK), jnp.int32)
            for r in range(KEEP):
                chosen = jnp.where(rows == r, index_ref[0, j, r], chosen)
            onehot = (chosen == lanes).astype(f32).astype(bf16)
            columns = pl.ds(pl.multiple_of(j * HD, HD), HD)
            keys = keys_ref[:, columns]
            values = values_ref[:, columns]
            key_rows = jnp.dot(onehot, keys, preferred_element_type=f32)
            value_rows = jnp.dot(onehot, values, preferred_element_type=f32)
            out_ref[h, :PAIR] = jnp.concatenate([key_rows, value_rows], axis=0).astype(bf16)
            out_ref[h, PAIR : PAIR + TOK] = keys
            out_ref[h, PAIR + TOK :] = values


def pick(block, keep_index, keys, values):
    shape = jax.ShapeDtypeStruct((HALF, PAIR + 2 * TOK, HD), bf16)
    return pl.pallas_call(
        pick_kernel,
        in_specs=[in_smem, in_smem, in_vmem, in_vmem],
        out_specs=(in_vmem, in_vmem),
        out_shape=(shape, shape),
    )(block, keep_index, keys, values)


def first_kernel(block_ref, mine_ref, came_ref, out_ref):
    core = block_ref[0] % NC
    for h in range(HALF):
        mine = mine_ref[h, :PAIR].astype(f32)
        came = came_ref[h, :PAIR].astype(f32)
        low = jnp.where(core == 0, mine, came)
        high = jnp.where(core == 0, came, mine)
        keys = jnp.concatenate([low[:KEEP], high[:KEEP]], axis=0).astype(bf16)
        values = jnp.concatenate([low[KEEP:], high[KEEP:]], axis=0).astype(bf16)
        for k in range(FIRST):
            out_ref[k, 2 * h * PAIR : (2 * h + 1) * PAIR] = keys
            out_ref[k, (2 * h + 1) * PAIR : (2 * h + 2) * PAIR] = values

    def pieces(ref):
        each = FIRST // HALF
        for k in range(FIRST):
            at = PAIR + (k % each) * PIECE
            out_ref[k, KEPT_ROWS:] = ref[k // each, at : at + PIECE]

    pl.when(core == 0)(lambda: pieces(mine_ref))
    pl.when(core != 0)(lambda: pieces(came_ref))


def second_kernel(in_ref, out_ref):
    for s in range(SECOND):
        for m in range(FIRST):
            for part in range(HALF * 2):
                at = part * CHUNK + m * PAIR
                out_ref[s, at : at + PAIR] = in_ref[m, part * PAIR : (part + 1) * PAIR]
        out_ref[s, HALF * 2 * CHUNK :] = in_ref[0, KEPT_ROWS:]


def attend_kernel(with_far, with_anchor, with_prior, with_own, other, *refs):
    refs = list(refs)
    take = lambda on: refs.pop(0) if on else None
    block_ref, q_ref, k_ref, v_ref = (take(True) for _ in range(4))
    far_ref, anchor_ref = take(with_far), take(with_anchor)
    prior_ref, prior_state_ref = take(with_prior), take(with_prior)
    if with_anchor and with_far:
        take(True)
    partial = not with_anchor
    out_ref, state_ref = take(True), take(partial)
    key_rows, value_rows, scratch = refs
    block = block_ref[0]
    head = pl.program_id(0)
    source = 1 - block % NC if other else block % NC
    first_key = k_ref[0:1, :]
    anchor_at = FAR if with_far else 0
    own_at = anchor_at + (TOK if with_anchor else 0)
    total_keys = own_at + (TOK if with_own else 0)

    @pl.when(head == 0)
    def _():
        if with_far:
            rows = lax.broadcasted_iota(jnp.int32, (CHUNK, HD), 0)
            u, zh, half = rows // (4 * PAIR), (rows // PAIR) % 4, (rows // KEEP) % NC
            step_u = jnp.where(source == 0, NZ * NC, NY * NZ * NC)
            step_a = jnp.where(source == 0, NY * NZ * NC, NZ * NC)
            sign = jnp.where(source == 0, 1, -1)
            for zl in range(2):
                base = u * step_u + ((2 * zh + sign * zl) % NZ) * NC + half
                for a in range(4):
                    owner = base + a * step_a
                    valid = ((owner >= 1) & (owner < block)).astype(f32).astype(bf16)
                    at = (a * 2 + zl) * CHUNK
                    value_rows[at : at + CHUNK, HD:] = valid
        if with_anchor:
            valid = jnp.where(block > 0, jnp.ones((TOK, HD), f32), 0.0).astype(bf16)
            value_rows[anchor_at : anchor_at + TOK, HD:] = valid
        if with_own:
            value_rows[own_at:total_keys, HD:] = jnp.ones((TOK, HD), bf16)

    def put(at, count, keys, values):
        valid = value_rows[at : at + count, HD:]
        spare = jnp.ones((count, HD), bf16) - valid
        key_rows[at : at + count, :] = keys * valid + first_key * spare
        value_rows[at : at + count, :HD] = values * valid

    if with_far:
        at_head = pl.multiple_of(head * 2 * CHUNK, 2 * CHUNK)
        for s in range(SECOND):
            put(
                s * CHUNK,
                CHUNK,
                far_ref[s, pl.ds(at_head, CHUNK), :],
                far_ref[s, pl.ds(at_head + CHUNK, CHUNK), :],
            )
    if with_anchor:
        pieces = TOK // PIECE
        for i in range(pieces):
            put(
                anchor_at + i * PIECE,
                PIECE,
                anchor_ref[head * 2 * pieces + i],
                anchor_ref[head * 2 * pieces + pieces + i],
            )
    if with_own:
        key_rows[own_at:total_keys, :] = k_ref[...]
        value_rows[own_at:total_keys, :HD] = v_ref[...]
        causal = lax.broadcasted_iota(jnp.int32, (TOK, TOK), 1) <= lax.broadcasted_iota(
            jnp.int32, (TOK, TOK), 0
        )

    def scores(g):
        found = lax.dot_general(
            q_ref[:, g * HD : (g + 1) * HD],
            key_rows[:total_keys, :],
            (((1,), (1,)), ((), ())),
            preferred_element_type=f32,
        )
        if with_own:
            scratch[g % 2, :, :own_at] = found[:, :own_at]
            scratch[g % 2, :, own_at:total_keys] = jnp.where(causal, found[:, own_at:], -1e30)
        else:
            scratch[g % 2, :, :total_keys] = found

    low_lanes = lax.broadcasted_iota(jnp.int32, (TOK, HD), 1) < HD // 2
    scores(0)
    for g in range(GROUP):
        if g + 1 < GROUP:
            scores(g + 1)
        columns = slice(g * HD, (g + 1) * HD)
        found = scratch[g % 2, :, :total_keys]
        highest = jnp.max(found, axis=1, keepdims=True)
        if with_prior:
            state = prior_state_ref[:, columns]
            prior_highest, prior_total = state[:, :1], state[:, HD - 1 :]
            highest = jnp.maximum(highest, prior_highest)
        weights = jnp.exp2((found - highest) * EXP2_SCALE).astype(bf16)
        summed = jnp.dot(weights, value_rows[:total_keys, :], preferred_element_type=f32)
        top, total = summed[:, :HD], summed[:, HD:]
        if with_prior:
            shrink = jnp.exp2((prior_highest - highest) * EXP2_SCALE)
            top = top + prior_ref[:, columns] * shrink
            total = total + prior_total * shrink
        if partial:
            out_ref[:, columns] = top
            state_ref[:, columns] = jnp.where(low_lanes, highest, total)
        else:
            out_ref[:, columns] = (top / total).astype(bf16)


def attend(block, queries, keys, values, far, anchor, prior, out, other):
    with_far, with_anchor, with_prior = far is not None, anchor is not None, prior is not None
    with_own = with_far

    def heads(i, block_ref):
        core = block_ref[0] % NC
        return (0, (1 - core if other else core) * HALF + i)

    wide = pl.BlockSpec((TOK, GROUP * HD), heads)
    local = pl.BlockSpec((TOK, GROUP * HD), lambda i, block_ref: (0, i))
    narrow = pl.BlockSpec((TOK, HD), heads)
    operands, in_specs, aliases = [queries, keys, values], [wide, narrow, narrow], {}
    if with_far:
        operands.append(far)
        in_specs.append(in_vmem)
    if with_anchor:
        operands.append(anchor)
        in_specs.append(in_vmem)
    if with_prior:
        operands += prior
        in_specs += [local, local]
    if out is not None:
        operands.append(out)
        in_specs.append(pl.BlockSpec(memory_space=pl.ANY))
        aliases = {len(operands): 0}
    if with_anchor:
        out_shape = jax.ShapeDtypeStruct((TOK, QH * HD), bf16)
        out_specs = wide
    else:
        out_shape = (jax.ShapeDtypeStruct((TOK, HALF * GROUP * HD), f32),) * 2
        out_specs = (local, local)
    rows = (FAR + TOK if with_far else 0) + (TOK if with_anchor else 0)
    work = HALF * GROUP * TOK * rows
    return pl.pallas_call(
        functools.partial(attend_kernel, with_far, with_anchor, with_prior, with_own, other),
        grid_spec=pltpu.PrefetchScalarGridSpec(
            num_scalar_prefetch=1,
            grid=(HALF,),
            in_specs=in_specs,
            out_specs=out_specs,
            scratch_shapes=[
                pltpu.VMEM((rows, HD), bf16),
                pltpu.VMEM((rows, 2 * HD), bf16),
                pltpu.VMEM((2, TOK, rows), f32),
            ],
        ),
        out_shape=out_shape,
        input_output_aliases=aliases,
        compiler_params=pltpu.CompilerParams(vmem_limit_bytes=VMEM_BYTES),
        cost_estimate=pl.CostEstimate(
            flops=4 * work * HD, bytes_accessed=4 * 1024 * 1024, transcendentals=work
        ),
    )(block, *operands)


def on_device(queries, keys, values, keep_index):
    block = lax.axis_index("d").astype(jnp.int32).reshape(1)
    swap = functools.partial(
        lax.ppermute, axis_name="d", perm=[(i, i ^ 1) for i in range(DEVICES)]
    )

    def gather(slots, groups):
        return lax.all_to_all(slots, "d", 0, 0, tiled=True, axis_index_groups=groups)

    mine, sent = pick(block, keep_index, keys, values)
    came = swap(sent)
    slots = pl.pallas_call(
        first_kernel,
        in_specs=[in_smem, in_vmem, in_vmem],
        out_specs=in_vmem,
        out_shape=jax.ShapeDtypeStruct((FIRST, KEPT_ROWS + PIECE, HD), bf16),
    )(block, mine, came)
    near = gather(slots, first_groups())
    slots = pl.pallas_call(
        second_kernel,
        in_specs=[in_vmem],
        out_specs=in_vmem,
        out_shape=jax.ShapeDtypeStruct((SECOND, SLOT, HD), bf16),
    )(near)
    far = gather(slots, second_groups())
    far_other = swap(far)
    piece = far[:1, HALF * 2 * CHUNK :]
    anchor = gather(jnp.tile(piece, (FIRST, 1, 1)), first_groups())
    anchor_other = swap(anchor)

    arrays = (block, queries, keys, values)
    prior = attend(*arrays, far, None, None, None, False)
    out = attend(*arrays, None, anchor, prior, None, False)
    return attend(*arrays, far_other, anchor_other, None, out, True)


def solution(mesh):
    line = Mesh(mesh.devices.reshape(DEVICES), ("d",))
    return jax.shard_map(
        on_device,
        mesh=line,
        in_specs=(P("d", None), P("d", None), P("d", None), P("d", None, None)),
        out_specs=P("d", None),
        check_vma=False,
    )
```

```python
import functools
import math

import jax
import jax.numpy as jnp
from jax import lax
from jax.experimental import pallas as pl
from jax.experimental.pallas import tpu as pltpu
from jax.sharding import Mesh, PartitionSpec as P

QH = 32
KVH = 4
HD = 128
KEEP = 8
TOK = 128
GROUP = QH // KVH
NX, NY, NZ, NC = 4, 4, 8, 2
DEVICES = NX * NY * NZ * NC
HALF = KVH // NC
FIRST = 16
SECOND = 8
PAIR = NC * KEEP
KEPT_ROWS = HALF * 2 * PAIR
CHUNK = FIRST * PAIR
PIECE = HALF * 2 * TOK // SECOND
SLOT = HALF * 2 * CHUNK + PIECE
PLANE = NY * NZ * NC * KEEP
PART = 4 * PAIR
EXP2_SCALE = math.log2(math.e) / math.sqrt(HD)
MIB = 1024 * 1024

bf16 = jnp.bfloat16
f32 = jnp.float32
in_smem = pl.BlockSpec(memory_space=pltpu.SMEM)
in_vmem = pl.BlockSpec(memory_space=pltpu.VMEM)


def at(x, y, z, core):
    return ((x * NY + y) * NZ + z) * NC + core


def device(core, a, u, zh, zl):
    x, y = (a, u) if core == 0 else (u, a)
    z = (2 * zh + zl) % NZ if core == 0 else (2 * zh - zl) % NZ
    return at(x, y, z, core)


def first_groups():
    return [
        [device(c, a, u, zh, zl) for u in range(4) for zh in range(4)]
        for c in range(2)
        for a in range(4)
        for zl in range(2)
    ]


def second_groups():
    return [
        [device(c, a, u, zh, zl) for a in range(4) for zl in range(2)]
        for c in range(2)
        for u in range(4)
        for zh in range(4)
    ]


def pick_kernel(block_ref, index_ref, keys_ref, values_ref, mine_ref, sent_ref, held_ref, lent_ref):
    core = block_ref[0] % NC
    rows = lax.broadcasted_iota(jnp.int32, (KEEP, TOK), 0)
    lanes = lax.broadcasted_iota(jnp.int32, (KEEP, TOK), 1)
    for out_ref, block_out_ref, owner in (
        (sent_ref, lent_ref, 1 - core),
        (mine_ref, held_ref, core),
    ):
        for h in range(HALF):
            j = owner * HALF + h
            chosen = jnp.zeros((KEEP, TOK), jnp.int32)
            for r in range(KEEP):
                chosen = jnp.where(rows == r, index_ref[0, j, r], chosen)
            onehot = (chosen == lanes).astype(f32).astype(bf16)
            columns = pl.ds(pl.multiple_of(j * HD, HD), HD)
            keys, values = keys_ref[:, columns], values_ref[:, columns]
            key_rows = jnp.dot(onehot, keys, preferred_element_type=f32)
            value_rows = jnp.dot(onehot, values, preferred_element_type=f32)
            out_ref[h] = jnp.concatenate([key_rows, value_rows], axis=0).astype(bf16)
            block_out_ref[2 * h * TOK : (2 * h + 1) * TOK] = keys
            block_out_ref[(2 * h + 1) * TOK : (2 * h + 2) * TOK] = values


def first_kernel(block_ref, mine_ref, came_ref, piece_ref, out_ref):
    core = block_ref[0] % NC
    for h in range(HALF):
        mine = mine_ref[h].astype(f32)
        came = came_ref[h].astype(f32)
        low = jnp.where(core == 0, mine, came)
        high = jnp.where(core == 0, came, mine)
        keys = jnp.concatenate([low[:KEEP], high[:KEEP]], axis=0).astype(bf16)
        values = jnp.concatenate([low[KEEP:], high[KEEP:]], axis=0).astype(bf16)
        for k in range(FIRST):
            out_ref[k, 2 * h * PAIR : (2 * h + 1) * PAIR] = keys
            out_ref[k, (2 * h + 1) * PAIR : (2 * h + 2) * PAIR] = values
    for k in range(FIRST):
        out_ref[k, KEPT_ROWS:] = piece_ref[0]


def second_kernel(in_ref, out_ref):
    for m in range(FIRST):
        for part in range(HALF * 2):
            rows = in_ref[m, part * PAIR : (part + 1) * PAIR]
            put = part * CHUNK + m * PAIR
            for s in range(SECOND):
                out_ref[s, put : put + PAIR] = rows
    for s in range(SECOND):
        out_ref[s, HALF * 2 * CHUNK :] = in_ref[0, KEPT_ROWS:]


def small_call(kernel, operands, in_specs, shapes, limit):
    return pl.pallas_call(
        kernel,
        in_specs=in_specs,
        out_specs=tuple(in_vmem for _ in shapes),
        out_shape=tuple(jax.ShapeDtypeStruct(s, bf16) for s in shapes),
        compiler_params=pltpu.CompilerParams(vmem_limit_bytes=limit * MIB),
    )(*operands)


def attend_kernel(other, block_ref, q_ref, k_ref, v_ref, far_ref, *refs):
    out_ref, key_rows, value_rows, even, odd = refs[-5:]
    block = block_ref[0]
    core = block % NC
    source = 1 - core if other else core
    first_head = source * HALF

    def columns_of(j, width):
        return pl.ds(pl.multiple_of(j * width, width), width)

    def run(planes):
        far = planes * PLANE
        keys = far + 2 * TOK

        def put(h, start, count, new_keys, new_values, valid):
            if valid is None:
                key_rows[h, start : start + count, :] = new_keys
                value_rows[h, start : start + count, :HD] = new_values
                value_rows[h, start : start + count, HD:] = jnp.ones((count, HD), bf16)
            else:
                first_key = k_ref[0:1, columns_of(first_head + h, HD)]
                spare = jnp.ones((count, HD), bf16) - valid
                key_rows[h, start : start + count, :] = new_keys * valid + first_key * spare
                value_rows[h, start : start + count, :HD] = new_values * valid
                value_rows[h, start : start + count, HD:] = valid

        def gather_rows(h):
            rows = lax.broadcasted_iota(jnp.int32, (PART, HD), 0)
            zh, half = rows // PAIR, (rows // KEEP) % NC
            for x in range(planes):
                for i in range(PLANE // PART):
                    slot = jnp.where(source == 0, 2 * x + i // 4, i)
                    row = jnp.where(source == 0, (i % 4) * PART, x * PART) + h * 2 * CHUNK
                    row = pl.multiple_of(row, PART)
                    valid = None
                    if x >= planes - 2 or (x == 0 and i == 0):
                        y = jnp.where(source == 0, i % 4, i // 2)
                        shift = jnp.where(source == 0, i // 4, NZ - i % 2)
                        owner = at(x, y, (2 * zh + shift) % NZ, half)
                        valid = ((owner >= 1) & (owner < block)).astype(f32).astype(bf16)
                    put(
                        h,
                        x * PLANE + i * PART,
                        PART,
                        far_ref[slot, pl.ds(row, PART), :],
                        far_ref[slot, pl.ds(pl.multiple_of(row + CHUNK, PART), PART), :],
                        valid,
                    )
            j = first_head + h
            valid = None
            if planes == 2:
                valid = jnp.where(block > 0, jnp.ones((PIECE, HD), f32), 0.0).astype(bf16)
            for i in range(TOK // PIECE):
                put(
                    h,
                    far + i * PIECE,
                    PIECE,
                    far_ref[h * 4 + i, HALF * 2 * CHUNK :, :],
                    far_ref[h * 4 + 2 + i, HALF * 2 * CHUNK :, :],
                    valid,
                )
            put(
                h,
                far + TOK,
                TOK,
                k_ref[:, columns_of(j, HD)],
                v_ref[:, columns_of(j, HD)],
                None,
            )

        causal = lax.broadcasted_iota(jnp.int32, (TOK, TOK), 1) <= lax.broadcasted_iota(
            jnp.int32, (TOK, TOK), 0
        )

        def scores(unit, held):
            found = lax.dot_general(
                q_ref[:, columns_of(first_head * GROUP + unit, HD)],
                key_rows[unit // GROUP, :keys, :],
                (((1,), (1,)), ((), ())),
                preferred_element_type=f32,
            )
            held[:, : keys - TOK] = found[:, : keys - TOK]
            held[:, keys - TOK : keys] = jnp.where(causal, found[:, keys - TOK :], -1e30)

        def finish(unit, held):
            found = held[:, :keys]
            highest = jnp.max(found, axis=1, keepdims=True)
            weights = jnp.exp2((found - highest) * EXP2_SCALE).astype(bf16)
            summed = jnp.dot(
                weights, value_rows[unit // GROUP, :keys, :], preferred_element_type=f32
            )
            out_ref[:, columns_of(unit, HD)] = (summed[:, :HD] / summed[:, HD:]).astype(bf16)

        units = HALF * GROUP
        gather_rows(0)
        scores(0, even)
        for unit in range(units):
            if unit == GROUP // 2:
                gather_rows(1)
            if unit + 1 < units:
                scores(unit + 1, even if unit % 2 else odd)
            finish(unit, odd if unit % 2 else even)

    near = block // (NY * NZ * NC) < NX // 2
    pl.when(near)(functools.partial(run, NX // 2))
    pl.when(jnp.logical_not(near))(functools.partial(run, NX))


def attend(block, queries, keys, values, far, out, other):
    def half(i, block_ref):
        core = block_ref[0] % NC
        return (0, 1 - core if other else core)

    operands = [queries, keys, values, far]
    in_specs = [in_vmem] * len(operands)
    aliases = {}
    if out is not None:
        operands.append(out)
        in_specs.append(pl.BlockSpec(memory_space=pl.ANY))
        aliases = {len(operands): 0}
    rows = NX * PLANE + 2 * TOK
    work = HALF * GROUP * TOK * rows
    return pl.pallas_call(
        functools.partial(attend_kernel, other),
        grid_spec=pltpu.PrefetchScalarGridSpec(
            num_scalar_prefetch=1,
            grid=(1,),
            in_specs=in_specs,
            out_specs=pl.BlockSpec((TOK, HALF * GROUP * HD), half),
            scratch_shapes=[
                pltpu.VMEM((HALF, rows, HD), bf16),
                pltpu.VMEM((HALF, rows, 2 * HD), bf16),
                pltpu.VMEM((TOK, rows), f32),
                pltpu.VMEM((TOK, rows), f32),
            ],
        ),
        out_shape=jax.ShapeDtypeStruct((TOK, QH * HD), bf16),
        input_output_aliases=aliases,
        compiler_params=pltpu.CompilerParams(vmem_limit_bytes=32 * MIB),
        cost_estimate=pl.CostEstimate(
            flops=4 * work * HD, bytes_accessed=4 * MIB, transcendentals=work
        ),
    )(block, *operands)


def on_device(queries, keys, values, keep_index):
    me = lax.axis_index("d")
    block = me.astype(jnp.int32).reshape(1)
    swap = functools.partial(
        lax.ppermute, axis_name="d", perm=[(i, i ^ 1) for i in range(DEVICES)]
    )

    def gather(slots, groups):
        return lax.all_to_all(slots, "d", 0, 0, tiled=True, axis_index_groups=groups)

    kept, own = (HALF, PAIR, HD), (HALF * 2 * TOK, HD)
    mine, sent, held, lent = small_call(
        pick_kernel,
        (block, keep_index, keys, values),
        [in_smem, in_smem, in_vmem, in_vmem],
        (kept, kept, own, own),
        60,
    )
    lent = lax.ppermute(lent, "d", [(0, 1)])
    anchor = jnp.where(me % NC == 0, held, lent)
    pieces = gather(anchor.reshape(SECOND, PIECE, HD), second_groups())
    (slots,) = small_call(
        first_kernel,
        (block, mine, swap(sent), pieces),
        [in_smem, in_vmem, in_vmem, in_vmem],
        ((FIRST, KEPT_ROWS + PIECE, HD),),
        4,
    )
    near = gather(slots, first_groups())
    (slots,) = small_call(second_kernel, (near,), [in_vmem], ((SECOND, SLOT, HD),), 8)
    far = gather(slots, second_groups())
    far_other = swap(far)

    out = attend(block, queries, keys, values, far, None, False)
    return attend(block, queries, keys, values, far_other, out, True)


def solution(mesh):
    line = Mesh(mesh.devices.reshape(DEVICES), ("d",))
    return jax.shard_map(
        on_device,
        mesh=line,
        in_specs=(P("d", None), P("d", None), P("d", None), P("d", None, None)),
        out_specs=P("d", None),
        check_vma=False,
    )
```

```python
import functools
import math

import jax
import jax.numpy as jnp
from jax import lax
from jax.experimental import pallas as pl
from jax.experimental.pallas import tpu as pltpu
from jax.sharding import Mesh, PartitionSpec as P

QH = 32
KVH = 4
HD = 128
KEEP = 8
TOK = 128
GROUP = QH // KVH
NX, NY, NZ, NC = 4, 4, 8, 2
DEVICES = NX * NY * NZ * NC
HALF = KVH // NC
FIRST = 16
SECOND = 8
PAIR = NC * KEEP
KEPT = HALF * PAIR
KEPT_ROWS = HALF * 2 * PAIR
CHUNK = FIRST * PAIR
PIECE = HALF * 2 * TOK // SECOND
SLOT = HALF * 2 * CHUNK + PIECE
PLANE = NY * NZ * NC * KEEP
PART = 4 * PAIR
EXP2_SCALE = math.log2(math.e) / math.sqrt(HD)
MIB = 1024 * 1024

bf16 = jnp.bfloat16
f32 = jnp.float32
in_smem = pl.BlockSpec(memory_space=pltpu.SMEM)
in_vmem = pl.BlockSpec(memory_space=pltpu.VMEM)


def at(x, y, z, core):
    return ((x * NY + y) * NZ + z) * NC + core


def device(core, a, u, zh, zl):
    x, y = (a, u) if core == 0 else (u, a)
    z = (2 * zh + zl) % NZ if core == 0 else (2 * zh - zl) % NZ
    return at(x, y, z, core)


def first_groups():
    return [
        [device(c, a, u, zh, zl) for u in range(4) for zh in range(4)]
        for c in range(2)
        for a in range(4)
        for zl in range(2)
    ]


def second_groups():
    return [
        [device(c, a, u, zh, zl) for a in range(4) for zl in range(2)]
        for c in range(2)
        for u in range(4)
        for zh in range(4)
    ]


def pick_kernel(
    block_ref, index_hbm, keys_hbm, values_hbm, mine_ref, sent_ref, index_ref, keys_ref, values_ref, done
):
    copies = [
        pltpu.make_async_copy(source, target, done.at[i])
        for i, (source, target) in enumerate(
            ((index_hbm, index_ref), (keys_hbm, keys_ref), (values_hbm, values_ref))
        )
    ]
    for copy in copies:
        copy.start()
    for copy in copies:
        copy.wait()
    block = block_ref[0]
    core = block % NC
    rows = lax.broadcasted_iota(jnp.int32, (KEEP, TOK), 0)
    lanes = lax.broadcasted_iota(jnp.int32, (KEEP, TOK), 1)
    for out_ref, owner in ((sent_ref, 1 - core), (mine_ref, core)):
        for h in range(HALF):
            j = owner * HALF + h
            chosen = jnp.zeros((KEEP, TOK), jnp.int32)
            for r in range(KEEP):
                chosen = jnp.where(rows == r, index_ref[0, j, r], chosen)
            onehot = (chosen == lanes).astype(f32).astype(bf16)
            columns = pl.ds(pl.multiple_of(j * HD, HD), HD)
            keys, values = keys_ref[:, columns], values_ref[:, columns]
            key_rows = jnp.dot(onehot, keys, preferred_element_type=f32)
            value_rows = jnp.dot(onehot, values, preferred_element_type=f32)
            found = jnp.concatenate([key_rows, value_rows], axis=0).astype(bf16)
            out_ref[h * PAIR : (h + 1) * PAIR] = found
            whole = jnp.concatenate([keys, values], axis=0)
            put = KEPT + 2 * h * TOK
            out_ref[put : put + 2 * TOK] = jnp.where(block == 0, whole, jnp.zeros_like(whole))


def first_kernel(block_ref, mine_ref, came_ref, out_ref):
    core = block_ref[0] % NC
    for h in range(HALF):
        mine = mine_ref[h * PAIR : (h + 1) * PAIR].astype(f32)
        came = came_ref[h * PAIR : (h + 1) * PAIR].astype(f32)
        low = jnp.where(core == 0, mine, came)
        high = jnp.where(core == 0, came, mine)
        keys = jnp.concatenate([low[:KEEP], high[:KEEP]], axis=0).astype(bf16)
        values = jnp.concatenate([low[KEEP:], high[KEEP:]], axis=0).astype(bf16)
        for k in range(FIRST):
            out_ref[k, 2 * h * PAIR : (2 * h + 1) * PAIR] = keys
            out_ref[k, (2 * h + 1) * PAIR : (2 * h + 2) * PAIR] = values


def second_kernel(in_ref, piece_ref, out_ref):
    for m in range(FIRST):
        for part in range(HALF * 2):
            rows = in_ref[m, part * PAIR : (part + 1) * PAIR]
            put = part * CHUNK + m * PAIR
            for s in range(SECOND):
                out_ref[s, put : put + PAIR] = rows
    for s in range(SECOND):
        out_ref[s, HALF * 2 * CHUNK :] = piece_ref[...]


def small_call(kernel, operands, in_specs, shapes, limit, scratch=()):
    return pl.pallas_call(
        kernel,
        in_specs=in_specs,
        out_specs=tuple(in_vmem for _ in shapes),
        out_shape=tuple(jax.ShapeDtypeStruct(s, bf16) for s in shapes),
        scratch_shapes=scratch,
        compiler_params=pltpu.CompilerParams(vmem_limit_bytes=limit * MIB),
    )(*operands)


def attend_kernel(other, block_ref, q_ref, k_ref, v_ref, far_ref, *refs):
    out_ref, key_rows, value_rows, even, odd = refs[-5:]
    block = block_ref[0]
    core = block % NC
    source = 1 - core if other else core
    first_head = source * HALF

    def columns_of(j, width):
        return pl.ds(pl.multiple_of(j * width, width), width)

    def run(full, planes):
        far = planes * PLANE
        keys = far + 2 * TOK

        def put(h, start, count, new_keys, new_values, valid):
            if valid is None:
                key_rows[h, start : start + count, :] = new_keys
                value_rows[h, start : start + count, :HD] = new_values
                value_rows[h, start : start + count, HD:] = jnp.ones((count, HD), bf16)
            else:
                first_key = k_ref[0:1, columns_of(first_head + h, HD)]
                spare = jnp.ones((count, HD), bf16) - valid
                key_rows[h, start : start + count, :] = new_keys * valid + first_key * spare
                value_rows[h, start : start + count, :HD] = new_values * valid
                value_rows[h, start : start + count, HD:] = valid

        def gather_rows(h):
            rows = lax.broadcasted_iota(jnp.int32, (PART, HD), 0)
            zh, half = rows // PAIR, (rows // KEEP) % NC
            for x in range(planes):
                for i in range(PLANE // PART):
                    slot = jnp.where(source == 0, 2 * x + i // 4, i)
                    row = jnp.where(source == 0, (i % 4) * PART, x * PART) + h * 2 * CHUNK
                    row = pl.multiple_of(row, PART)
                    valid = None
                    if x >= full or (x == 0 and i == 0):
                        y = jnp.where(source == 0, i % 4, i // 2)
                        shift = jnp.where(source == 0, i // 4, NZ - i % 2)
                        owner = at(x, y, (2 * zh + shift) % NZ, half)
                        valid = ((owner >= 1) & (owner < block)).astype(f32).astype(bf16)
                    put(
                        h,
                        x * PLANE + i * PART,
                        PART,
                        far_ref[slot, pl.ds(row, PART), :],
                        far_ref[slot, pl.ds(pl.multiple_of(row + CHUNK, PART), PART), :],
                        valid,
                    )
            j = first_head + h
            valid = None
            if full == 0:
                valid = jnp.where(block > 0, jnp.ones((PIECE, HD), f32), 0.0).astype(bf16)
            for i in range(TOK // PIECE):
                put(
                    h,
                    far + i * PIECE,
                    PIECE,
                    far_ref[h * 4 + i, HALF * 2 * CHUNK :, :],
                    far_ref[h * 4 + 2 + i, HALF * 2 * CHUNK :, :],
                    valid,
                )
            put(
                h,
                far + TOK,
                TOK,
                k_ref[:, columns_of(j, HD)],
                v_ref[:, columns_of(j, HD)],
                None,
            )

        causal = lax.broadcasted_iota(jnp.int32, (TOK, TOK), 1) <= lax.broadcasted_iota(
            jnp.int32, (TOK, TOK), 0
        )

        def scores(unit, held):
            found = lax.dot_general(
                q_ref[:, columns_of(first_head * GROUP + unit, HD)],
                key_rows[unit // GROUP, :keys, :],
                (((1,), (1,)), ((), ())),
                preferred_element_type=f32,
            )
            held[:, : keys - TOK] = found[:, : keys - TOK]
            held[:, keys - TOK : keys] = jnp.where(causal, found[:, keys - TOK :], -1e30)

        def finish(unit, held):
            found = held[:, :keys]
            highest = jnp.max(found, axis=1, keepdims=True)
            weights = jnp.exp2((found - highest) * EXP2_SCALE).astype(bf16)
            summed = jnp.dot(
                weights, value_rows[unit // GROUP, :keys, :], preferred_element_type=f32
            )
            out_ref[:, columns_of(unit, HD)] = (summed[:, :HD] / summed[:, HD:]).astype(bf16)

        units = HALF * GROUP
        gather_rows(0)
        scores(0, even)
        for unit in range(units):
            if unit == GROUP // 2:
                gather_rows(1)
            if unit + 1 < units:
                scores(unit + 1, even if unit % 2 else odd)
            finish(unit, odd if unit % 2 else even)

    own_plane = block // (NY * NZ * NC)
    for low, high in ((0, 1), (1, 2), (2, 4)):
        here = (own_plane >= low) & (own_plane < high)
        pl.when(here)(functools.partial(run, low, high))


def attend(block, queries, keys, values, far, out, other):
    def half(i, block_ref):
        core = block_ref[0] % NC
        return (0, 1 - core if other else core)

    operands = [queries, keys, values, far]
    in_specs = [in_vmem] * len(operands)
    aliases = {}
    if out is not None:
        operands.append(out)
        in_specs.append(pl.BlockSpec(memory_space=pl.ANY))
        aliases = {len(operands): 0}
    rows = NX * PLANE + 2 * TOK
    work = HALF * GROUP * TOK * rows
    return pl.pallas_call(
        functools.partial(attend_kernel, other),
        grid_spec=pltpu.PrefetchScalarGridSpec(
            num_scalar_prefetch=1,
            grid=(1,),
            in_specs=in_specs,
            out_specs=pl.BlockSpec((TOK, HALF * GROUP * HD), half),
            scratch_shapes=[
                pltpu.VMEM((HALF, rows, HD), bf16),
                pltpu.VMEM((HALF, rows, 2 * HD), bf16),
                pltpu.VMEM((TOK, rows), f32),
                pltpu.VMEM((TOK, rows), f32),
            ],
        ),
        out_shape=jax.ShapeDtypeStruct((TOK, QH * HD), bf16),
        input_output_aliases=aliases,
        compiler_params=pltpu.CompilerParams(vmem_limit_bytes=32 * MIB),
        cost_estimate=pl.CostEstimate(
            flops=4 * work * HD, bytes_accessed=4 * MIB, transcendentals=work
        ),
    )(block, *operands)


def send(rows, pairs):
    return lax.ppermute(rows, "d", pairs)


def anchor_at_base(held):
    pieces = held[: 2 * PIECE]
    for a in range(1, 4):
        pairs = [(device(c, 0, 0, 0, 0), device(c, a, 0, 0, 0)) for c in range(NC)]
        pieces = pieces + send(held[2 * a * PIECE : 2 * (a + 1) * PIECE], pairs)
    steps = (
        [(device(c, a, 0, 0, 0), device(c, a, u, 0, 0)) for c in range(NC) for a in range(4)]
        for u in range(1, 4)
    )
    return sum((send(pieces, pairs) for pairs in steps), pieces)


def anchor_along_z(pieces):
    lines = [(c, a, u) for c in range(NC) for a in range(4) for u in range(4)]
    other = send(
        pieces[PIECE:], [(device(*line, 0, 0), device(*line, 0, 1)) for line in lines]
    )
    piece = pieces[:PIECE] + other
    steps = (
        [(device(*line, 0, zl), device(*line, zh, zl)) for line in lines for zl in range(2)]
        for zh in range(1, 4)
    )
    return sum((send(piece, pairs) for pairs in steps), piece)


def on_device(queries, keys, values, keep_index):
    me = lax.axis_index("d")
    block = me.astype(jnp.int32).reshape(1)
    swap = functools.partial(
        lax.ppermute, axis_name="d", perm=[(i, i ^ 1) for i in range(DEVICES)]
    )

    def gather(slots, groups):
        return lax.all_to_all(slots, "d", 0, 0, tiled=True, axis_index_groups=groups)

    given = (KEPT + HALF * 2 * TOK, HD)
    mine, sent = small_call(
        pick_kernel,
        (block, keep_index, keys, values),
        [in_smem] + [pl.BlockSpec(memory_space=pl.ANY)] * 3,
        (given, given),
        4,
        (
            pltpu.SMEM(keep_index.shape, jnp.int32),
            pltpu.VMEM(keys.shape, bf16),
            pltpu.VMEM(values.shape, bf16),
            pltpu.SemaphoreType.DMA((3,)),
        ),
    )
    came = swap(sent)
    base = anchor_at_base(mine[KEPT:] + came[KEPT:])
    (slots,) = small_call(
        first_kernel,
        (block, mine, came),
        [in_smem, in_vmem, in_vmem],
        ((FIRST, KEPT_ROWS, HD),),
        4,
    )
    near = gather(slots, first_groups())
    (slots,) = small_call(second_kernel, (near, anchor_along_z(base)), [in_vmem, in_vmem], ((SECOND, SLOT, HD),), 8)
    far = gather(slots, second_groups())
    far_other = swap(far)

    out = attend(block, queries, keys, values, far, None, False)
    return attend(block, queries, keys, values, far_other, out, True)


def solution(mesh):
    line = Mesh(mesh.devices.reshape(DEVICES), ("d",))
    return jax.shard_map(
        on_device,
        mesh=line,
        in_specs=(P("d", None), P("d", None), P("d", None), P("d", None, None)),
        out_specs=P("d", None),
        check_vma=False,
    )
```

```python
import functools
import math

import jax
import jax.numpy as jnp
from jax import lax
from jax.experimental import pallas as pl
from jax.experimental.pallas import tpu as pltpu
from jax.sharding import Mesh, PartitionSpec as P

QH = 32
KVH = 4
HD = 128
KEEP = 8
TOK = 128
GROUP = QH // KVH
NX, NY, NZ, NC = 4, 4, 8, 2
DEVICES = NX * NY * NZ * NC
HALF = KVH // NC
FIRST = 16
SECOND = 8
PAIR = NC * KEEP
KEPT = HALF * PAIR
KEPT_ROWS = HALF * 2 * PAIR
CHUNK = FIRST * PAIR
PIECE = HALF * 2 * TOK // SECOND
SLOT = HALF * 2 * CHUNK + PIECE
PLANE = NY * NZ * NC * KEEP
PART = 4 * PAIR
EXP2_SCALE = math.log2(math.e) / math.sqrt(HD)
MIB = 1024 * 1024

bf16 = jnp.bfloat16
f32 = jnp.float32
in_smem = pl.BlockSpec(memory_space=pltpu.SMEM)
in_vmem = pl.BlockSpec(memory_space=pltpu.VMEM)


def at(x, y, z, core):
    return ((x * NY + y) * NZ + z) * NC + core


def device(core, a, u, zh, zl):
    x, y = (a, u) if core == 0 else (u, a)
    z = (2 * zh + zl) % NZ if core == 0 else (2 * zh - zl) % NZ
    return at(x, y, z, core)


def first_groups():
    return [
        [device(c, a, u, zh, zl) for u in range(4) for zh in range(4)]
        for c in range(2)
        for a in range(4)
        for zl in range(2)
    ]


def second_groups():
    return [
        [device(c, a, u, zh, zl) for a in range(4) for zl in range(2)]
        for c in range(2)
        for u in range(4)
        for zh in range(4)
    ]


def pick_kernel(block_ref, index_ref, both_ref, mine_ref, sent_ref):
    block = block_ref[0]
    core = block % NC
    rows = lax.broadcasted_iota(jnp.int32, (KEEP, TOK), 0)
    lanes = lax.broadcasted_iota(jnp.int32, (KEEP, TOK), 1)
    for out_ref, owner in ((sent_ref, 1 - core), (mine_ref, core)):
        for h in range(HALF):
            j = owner * HALF + h
            chosen = jnp.zeros((KEEP, TOK), jnp.int32)
            for r in range(KEEP):
                chosen = jnp.where(rows == r, index_ref[0, j, r], chosen)
            onehot = (chosen == lanes).astype(f32).astype(bf16)
            keys = both_ref[:, pl.ds(pl.multiple_of(j * HD, HD), HD)]
            values = both_ref[:, pl.ds(pl.multiple_of((KVH + j) * HD, HD), HD)]
            key_rows = jnp.dot(onehot, keys, preferred_element_type=f32)
            value_rows = jnp.dot(onehot, values, preferred_element_type=f32)
            found = jnp.concatenate([key_rows, value_rows], axis=0).astype(bf16)
            out_ref[h * PAIR : (h + 1) * PAIR] = found
            whole = jnp.concatenate([keys, values], axis=0)
            put = KEPT + 2 * h * TOK
            out_ref[put : put + 2 * TOK] = jnp.where(block == 0, whole, jnp.zeros_like(whole))


def first_kernel(block_ref, mine_ref, came_ref, out_ref):
    core = block_ref[0] % NC
    for h in range(HALF):
        mine = mine_ref[h * PAIR : (h + 1) * PAIR].astype(f32)
        came = came_ref[h * PAIR : (h + 1) * PAIR].astype(f32)
        low = jnp.where(core == 0, mine, came)
        high = jnp.where(core == 0, came, mine)
        keys = jnp.concatenate([low[:KEEP], high[:KEEP]], axis=0).astype(bf16)
        values = jnp.concatenate([low[KEEP:], high[KEEP:]], axis=0).astype(bf16)
        for k in range(FIRST):
            out_ref[k, 2 * h * PAIR : (2 * h + 1) * PAIR] = keys
            out_ref[k, (2 * h + 1) * PAIR : (2 * h + 2) * PAIR] = values


def second_kernel(in_ref, piece_ref, out_ref):
    for m in range(FIRST):
        for part in range(HALF * 2):
            rows = in_ref[m, part * PAIR : (part + 1) * PAIR]
            put = part * CHUNK + m * PAIR
            for s in range(SECOND):
                out_ref[s, put : put + PAIR] = rows
    for s in range(SECOND):
        out_ref[s, HALF * 2 * CHUNK :] = piece_ref[...]


def small_call(kernel, operands, in_specs, shapes, limit):
    return pl.pallas_call(
        kernel,
        in_specs=in_specs,
        out_specs=tuple(in_vmem for _ in shapes),
        out_shape=tuple(jax.ShapeDtypeStruct(s, bf16) for s in shapes),
        compiler_params=pltpu.CompilerParams(vmem_limit_bytes=limit * MIB),
    )(*operands)


def attend_kernel(other, block_ref, q_ref, k_ref, v_ref, far_ref, *refs):
    out_ref, key_rows, value_rows, even, odd, third = refs[-6:]
    block = block_ref[0]
    core = block % NC
    source = 1 - core if other else core
    first_head = source * HALF

    def columns_of(j, width):
        return pl.ds(pl.multiple_of(j * width, width), width)

    def run(full, planes):
        far = planes * PLANE
        keys = far + 2 * TOK

        def put(h, start, count, new_keys, new_values, valid):
            if valid is None:
                key_rows[h, start : start + count, :] = new_keys
                value_rows[h, start : start + count, :HD] = new_values
                value_rows[h, start : start + count, HD:] = jnp.ones((count, HD), bf16)
            else:
                first_key = k_ref[0:1, columns_of(first_head + h, HD)]
                spare = jnp.ones((count, HD), bf16) - valid
                key_rows[h, start : start + count, :] = new_keys * valid + first_key * spare
                value_rows[h, start : start + count, :HD] = new_values * valid
                value_rows[h, start : start + count, HD:] = valid

        def gather_rows(h):
            rows = lax.broadcasted_iota(jnp.int32, (PART, HD), 0)
            zh, half = rows // PAIR, (rows // KEEP) % NC
            for x in range(planes):
                for i in range(PLANE // PART):
                    slot = jnp.where(source == 0, 2 * x + i // 4, i)
                    row = jnp.where(source == 0, (i % 4) * PART, x * PART) + h * 2 * CHUNK
                    row = pl.multiple_of(row, PART)
                    valid = None
                    if x >= full or (x == 0 and i == 0):
                        y = jnp.where(source == 0, i % 4, i // 2)
                        shift = jnp.where(source == 0, i // 4, NZ - i % 2)
                        owner = at(x, y, (2 * zh + shift) % NZ, half)
                        valid = ((owner >= 1) & (owner < block)).astype(f32).astype(bf16)
                    put(
                        h,
                        x * PLANE + i * PART,
                        PART,
                        far_ref[slot, pl.ds(row, PART), :],
                        far_ref[slot, pl.ds(pl.multiple_of(row + CHUNK, PART), PART), :],
                        valid,
                    )
            j = first_head + h
            valid = None
            if full == 0:
                valid = jnp.where(block > 0, jnp.ones((PIECE, HD), f32), 0.0).astype(bf16)
            for i in range(TOK // PIECE):
                put(
                    h,
                    far + i * PIECE,
                    PIECE,
                    far_ref[2 * i + h, HALF * 2 * CHUNK :, :],
                    far_ref[2 * (i + 2) + h, HALF * 2 * CHUNK :, :],
                    valid,
                )
            put(
                h,
                far + TOK,
                TOK,
                k_ref[:, columns_of(j, HD)],
                v_ref[:, columns_of(j, HD)],
                None,
            )

        causal = lax.broadcasted_iota(jnp.int32, (TOK, TOK), 1) <= lax.broadcasted_iota(
            jnp.int32, (TOK, TOK), 0
        )

        def scores(unit, held):
            found = lax.dot_general(
                q_ref[:, columns_of(first_head * GROUP + unit, HD)],
                key_rows[unit // GROUP, :keys, :],
                (((1,), (1,)), ((), ())),
                preferred_element_type=f32,
            )
            held[:, : keys - TOK] = found[:, : keys - TOK]
            held[:, keys - TOK : keys] = jnp.where(causal, found[:, keys - TOK :], -1e30)

        def finish(unit, held):
            found = held[:, :keys]
            highest = jnp.max(found, axis=1, keepdims=True)
            weights = jnp.exp2((found - highest) * EXP2_SCALE).astype(bf16)
            summed = jnp.dot(
                weights, value_rows[unit // GROUP, :keys, :], preferred_element_type=f32
            )
            out_ref[:, columns_of(unit, HD)] = (summed[:, :HD] / summed[:, HD:]).astype(bf16)

        units = HALF * GROUP
        gather_rows(0)
        buffers = (even, odd, third)
        scores(0, even)
        scores(1, odd)
        for unit in range(units):
            if unit == GROUP // 2:
                gather_rows(1)
            if unit + 2 < units:
                scores(unit + 2, buffers[(unit + 2) % 3])
            finish(unit, buffers[unit % 3])

    own_plane = block // (NY * NZ * NC)
    for low, high in ((0, 1), (1, 2), (2, 4)):
        here = (own_plane >= low) & (own_plane < high)
        pl.when(here)(functools.partial(run, low, high))


def attend(block, queries, keys, values, far, out, other):
    def half(i, block_ref):
        core = block_ref[0] % NC
        return (0, 1 - core if other else core)

    operands = [queries, keys, values, far]
    in_specs = [in_vmem] * len(operands)
    aliases = {}
    if out is not None:
        operands.append(out)
        in_specs.append(pl.BlockSpec(memory_space=pl.ANY))
        aliases = {len(operands): 0}
    rows = NX * PLANE + 2 * TOK
    work = HALF * GROUP * TOK * rows
    return pl.pallas_call(
        functools.partial(attend_kernel, other),
        grid_spec=pltpu.PrefetchScalarGridSpec(
            num_scalar_prefetch=1,
            grid=(1,),
            in_specs=in_specs,
            out_specs=pl.BlockSpec((TOK, HALF * GROUP * HD), half),
            scratch_shapes=[
                pltpu.VMEM((HALF, rows, HD), bf16),
                pltpu.VMEM((HALF, rows, 2 * HD), bf16),
                pltpu.VMEM((TOK, rows), f32),
                pltpu.VMEM((TOK, rows), f32),
                pltpu.VMEM((TOK, rows), f32),
            ],
        ),
        out_shape=jax.ShapeDtypeStruct((TOK, QH * HD), bf16),
        input_output_aliases=aliases,
        compiler_params=pltpu.CompilerParams(vmem_limit_bytes=32 * MIB),
        cost_estimate=pl.CostEstimate(
            flops=4 * work * HD, bytes_accessed=4 * MIB, transcendentals=work
        ),
    )(block, *operands)


def send(rows, pairs):
    return lax.ppermute(rows, "d", pairs)


def anchor_over_second(held):
    half = HALF * TOK
    rows = held[:half] + send(
        held[half:], [(device(c, 0, 0, 0, 0), device(c, 0, 0, 0, 1)) for c in range(NC)]
    )
    steps = (
        [(device(c, 0, 0, 0, zl), device(c, a, 0, 0, zl)) for c in range(NC) for zl in range(2)]
        for a in range(1, 4)
    )
    pieces = (rows[a * PIECE : (a + 1) * PIECE] for a in range(1, 4))
    return sum((send(piece, pairs) for piece, pairs in zip(pieces, steps)), rows[:PIECE])


def anchor_over_first(piece):
    lines = [(c, a, zl) for c in range(NC) for a in range(4) for zl in range(2)]
    steps = (
        [(device(c, a, 0, 0, zl), device(c, a, u, 0, zl)) for c, a, zl in lines]
        for u in range(1, 4)
    )
    piece = sum((send(piece, pairs) for pairs in steps), piece)
    steps = (
        [(device(c, a, u, 0, zl), device(c, a, u, zh, zl)) for c, a, zl in lines for u in range(4)]
        for zh in range(1, 4)
    )
    return sum((send(piece, pairs) for pairs in steps), piece)


def on_device(queries, keys, values, keep_index):
    me = lax.axis_index("d")
    block = me.astype(jnp.int32).reshape(1)
    swap = functools.partial(
        lax.ppermute, axis_name="d", perm=[(i, i ^ 1) for i in range(DEVICES)]
    )

    def gather(slots, groups):
        return lax.all_to_all(slots, "d", 0, 0, tiled=True, axis_index_groups=groups)

    given = (KEPT + HALF * 2 * TOK, HD)
    mine, sent = small_call(
        pick_kernel,
        (block, keep_index, jnp.concatenate([keys, values], axis=1)),
        [in_smem, in_smem, in_vmem],
        (given, given),
        4,
    )
    came = swap(sent)
    base = anchor_over_second(mine[KEPT:] + came[KEPT:])
    (slots,) = small_call(
        first_kernel,
        (block, mine, came),
        [in_smem, in_vmem, in_vmem],
        ((FIRST, KEPT_ROWS, HD),),
        4,
    )
    near = gather(slots, first_groups())
    (slots,) = small_call(second_kernel, (near, anchor_over_first(base)), [in_vmem, in_vmem], ((SECOND, SLOT, HD),), 8)
    far = gather(slots, second_groups())
    far_other = swap(far)

    out = attend(block, queries, keys, values, far, None, False)
    return attend(block, queries, keys, values, far_other, out, True)


def solution(mesh):
    line = Mesh(mesh.devices.reshape(DEVICES), ("d",))
    return jax.shard_map(
        on_device,
        mesh=line,
        in_specs=(P("d", None), P("d", None), P("d", None), P("d", None, None)),
        out_specs=P("d", None),
        check_vma=False,
    )
```

```python
import functools
import math

import jax
import jax.numpy as jnp
from jax import lax
from jax.experimental import pallas as pl
from jax.experimental.pallas import tpu as pltpu
from jax.sharding import Mesh, PartitionSpec as P

QH = 32
KVH = 4
HD = 128
KEEP = 8
TOK = 128
GROUP = QH // KVH
NX, NY, NZ, NC = 4, 4, 8, 2
DEVICES = NX * NY * NZ * NC
HALF = KVH // NC
FIRST = 16
SECOND = 8
PAIR = NC * KEEP
KEPT = HALF * PAIR
KEPT_ROWS = HALF * 2 * PAIR
CHUNK = FIRST * PAIR
PIECE = HALF * 2 * TOK // SECOND
SLOT = HALF * 2 * CHUNK + PIECE
PLANE = NY * NZ * NC * KEEP
PART = 4 * PAIR
EXP2_SCALE = math.log2(math.e) / math.sqrt(HD)
MIB = 1024 * 1024

bf16 = jnp.bfloat16
f32 = jnp.float32
in_smem = pl.BlockSpec(memory_space=pltpu.SMEM)
in_vmem = pl.BlockSpec(memory_space=pltpu.VMEM)


def at(x, y, z, core):
    return ((x * NY + y) * NZ + z) * NC + core


def device(core, a, u, zh, zl):
    x, y = (a, u) if core == 0 else (u, a)
    z = (2 * zh + zl) % NZ if core == 0 else (2 * zh - zl) % NZ
    return at(x, y, z, core)


def first_groups():
    return [
        [device(c, a, u, zh, zl) for u in range(4) for zh in range(4)]
        for c in range(2)
        for a in range(4)
        for zl in range(2)
    ]


def second_groups():
    return [
        [device(c, a, u, zh, zl) for a in range(4) for zl in range(2)]
        for c in range(2)
        for u in range(4)
        for zh in range(4)
    ]


def pick_kernel(block_ref, index_ref, both_ref, mine_ref, sent_ref):
    block = block_ref[0]
    core = block % NC
    rows = lax.broadcasted_iota(jnp.int32, (KEEP, TOK), 0)
    lanes = lax.broadcasted_iota(jnp.int32, (KEEP, TOK), 1)
    for out_ref, owner in ((sent_ref, 1 - core), (mine_ref, core)):
        for h in range(HALF):
            j = owner * HALF + h
            chosen = jnp.zeros((KEEP, TOK), jnp.int32)
            for r in range(KEEP):
                chosen = jnp.where(rows == r, index_ref[0, j, r], chosen)
            onehot = (chosen == lanes).astype(f32).astype(bf16)
            keys = both_ref[:, pl.ds(pl.multiple_of(j * HD, HD), HD)]
            values = both_ref[:, pl.ds(pl.multiple_of((KVH + j) * HD, HD), HD)]
            key_rows = jnp.dot(onehot, keys, preferred_element_type=f32)
            value_rows = jnp.dot(onehot, values, preferred_element_type=f32)
            found = jnp.concatenate([key_rows, value_rows], axis=0).astype(bf16)
            out_ref[h * PAIR : (h + 1) * PAIR] = found
            whole = jnp.concatenate([keys, values], axis=0)
            put = KEPT + 2 * h * TOK
            out_ref[put : put + 2 * TOK] = jnp.where(block == 0, whole, jnp.zeros_like(whole))


def first_kernel(block_ref, mine_ref, came_ref, out_ref):
    core = block_ref[0] % NC
    for h in range(HALF):
        mine = mine_ref[h * PAIR : (h + 1) * PAIR].astype(f32)
        came = came_ref[h * PAIR : (h + 1) * PAIR].astype(f32)
        low = jnp.where(core == 0, mine, came)
        high = jnp.where(core == 0, came, mine)
        keys = jnp.concatenate([low[:KEEP], high[:KEEP]], axis=0).astype(bf16)
        values = jnp.concatenate([low[KEEP:], high[KEEP:]], axis=0).astype(bf16)
        for k in range(FIRST):
            out_ref[k, 2 * h * PAIR : (2 * h + 1) * PAIR] = keys
            out_ref[k, (2 * h + 1) * PAIR : (2 * h + 2) * PAIR] = values


def second_kernel(in_ref, piece_ref, out_ref):
    for m in range(FIRST):
        for part in range(HALF * 2):
            rows = in_ref[m, part * PAIR : (part + 1) * PAIR]
            put = part * CHUNK + m * PAIR
            for s in range(SECOND):
                out_ref[s, put : put + PAIR] = rows
    for s in range(SECOND):
        out_ref[s, HALF * 2 * CHUNK :] = piece_ref[...]


def small_call(kernel, operands, in_specs, shapes, limit):
    return pl.pallas_call(
        kernel,
        in_specs=in_specs,
        out_specs=tuple(in_vmem for _ in shapes),
        out_shape=tuple(jax.ShapeDtypeStruct(s, bf16) for s in shapes),
        compiler_params=pltpu.CompilerParams(vmem_limit_bytes=limit * MIB),
    )(*operands)


def attend_kernel(other, block_ref, q_ref, k_ref, v_ref, far_ref, *refs):
    out_ref, key_rows, value_rows, even, odd, third = refs[-6:]
    block = block_ref[0]
    core = block % NC
    source = 1 - core if other else core
    first_head = source * HALF

    def columns_of(j, width):
        return pl.ds(pl.multiple_of(j * width, width), width)

    def run(full, planes):
        far = planes * PLANE
        keys = far + 2 * TOK

        def put(h, start, count, new_keys, new_values, valid):
            if valid is None:
                key_rows[h, start : start + count, :] = new_keys
                value_rows[h, start : start + count, :HD] = new_values
                value_rows[h, start : start + count, HD:] = jnp.ones((count, HD), bf16)
            else:
                first_key = k_ref[0:1, columns_of(first_head + h, HD)]
                spare = jnp.ones((count, HD), bf16) - valid
                key_rows[h, start : start + count, :] = new_keys * valid + first_key * spare
                value_rows[h, start : start + count, :HD] = new_values * valid
                value_rows[h, start : start + count, HD:] = valid

        def gather_rows(h):
            rows = lax.broadcasted_iota(jnp.int32, (PART, HD), 0)
            zh, half = rows // PAIR, (rows // KEEP) % NC
            for x in range(planes):
                for i in range(PLANE // PART):
                    slot = jnp.where(source == 0, 2 * x + i // 4, i)
                    row = jnp.where(source == 0, (i % 4) * PART, x * PART) + h * 2 * CHUNK
                    row = pl.multiple_of(row, PART)
                    valid = None
                    if x >= full or (x == 0 and i == 0):
                        y = jnp.where(source == 0, i % 4, i // 2)
                        shift = jnp.where(source == 0, i // 4, NZ - i % 2)
                        owner = at(x, y, (2 * zh + shift) % NZ, half)
                        valid = ((owner >= 1) & (owner < block)).astype(f32).astype(bf16)
                    put(
                        h,
                        x * PLANE + i * PART,
                        PART,
                        far_ref[slot, pl.ds(row, PART), :],
                        far_ref[slot, pl.ds(pl.multiple_of(row + CHUNK, PART), PART), :],
                        valid,
                    )
            j = first_head + h
            valid = None
            if full == 0:
                valid = jnp.where(block > 0, jnp.ones((PIECE, HD), f32), 0.0).astype(bf16)
            for i in range(TOK // PIECE):
                put(
                    h,
                    far + i * PIECE,
                    PIECE,
                    far_ref[h * 4 + i, HALF * 2 * CHUNK :, :],
                    far_ref[h * 4 + 2 + i, HALF * 2 * CHUNK :, :],
                    valid,
                )
            put(
                h,
                far + TOK,
                TOK,
                k_ref[:, columns_of(j, HD)],
                v_ref[:, columns_of(j, HD)],
                None,
            )

        causal = lax.broadcasted_iota(jnp.int32, (TOK, TOK), 1) <= lax.broadcasted_iota(
            jnp.int32, (TOK, TOK), 0
        )

        def scores(unit, held):
            found = lax.dot_general(
                q_ref[:, columns_of(first_head * GROUP + unit, HD)],
                key_rows[unit // GROUP, :keys, :],
                (((1,), (1,)), ((), ())),
                preferred_element_type=f32,
            )
            held[:, : keys - TOK] = found[:, : keys - TOK]
            held[:, keys - TOK : keys] = jnp.where(causal, found[:, keys - TOK :], -1e30)

        def finish(unit, held):
            found = held[:, :keys]
            highest = jnp.max(found, axis=1, keepdims=True)
            weights = jnp.exp2((found - highest) * EXP2_SCALE).astype(bf16)
            summed = jnp.dot(
                weights, value_rows[unit // GROUP, :keys, :], preferred_element_type=f32
            )
            out_ref[:, columns_of(unit, HD)] = (summed[:, :HD] / summed[:, HD:]).astype(bf16)

        units = HALF * GROUP
        gather_rows(0)
        buffers = (even, odd, third)
        scores(0, even)
        scores(1, odd)
        for unit in range(units):
            if unit == GROUP // 2:
                gather_rows(1)
            if unit + 2 < units:
                scores(unit + 2, buffers[(unit + 2) % 3])
            finish(unit, buffers[unit % 3])

    own_plane = block // (NY * NZ * NC)
    for low, high in ((0, 1), (1, 2), (2, 4)):
        here = (own_plane >= low) & (own_plane < high)
        pl.when(here)(functools.partial(run, low, high))


def attend(block, queries, keys, values, far, out, other):
    def half(i, block_ref):
        core = block_ref[0] % NC
        return (0, 1 - core if other else core)

    operands = [queries, keys, values, far]
    in_specs = [in_vmem] * len(operands)
    aliases = {}
    if out is not None:
        operands.append(out)
        in_specs.append(pl.BlockSpec(memory_space=pl.ANY))
        aliases = {len(operands): 0}
    rows = NX * PLANE + 2 * TOK
    work = HALF * GROUP * TOK * rows
    return pl.pallas_call(
        functools.partial(attend_kernel, other),
        grid_spec=pltpu.PrefetchScalarGridSpec(
            num_scalar_prefetch=1,
            grid=(1,),
            in_specs=in_specs,
            out_specs=pl.BlockSpec((TOK, HALF * GROUP * HD), half),
            scratch_shapes=[
                pltpu.VMEM((HALF, rows, HD), bf16),
                pltpu.VMEM((HALF, rows, 2 * HD), bf16),
                pltpu.VMEM((TOK, rows), f32),
                pltpu.VMEM((TOK, rows), f32),
                pltpu.VMEM((TOK, rows), f32),
            ],
        ),
        out_shape=jax.ShapeDtypeStruct((TOK, QH * HD), bf16),
        input_output_aliases=aliases,
        compiler_params=pltpu.CompilerParams(vmem_limit_bytes=32 * MIB),
        cost_estimate=pl.CostEstimate(
            flops=4 * work * HD, bytes_accessed=4 * MIB, transcendentals=work
        ),
    )(block, *operands)


def send(rows, pairs):
    return lax.ppermute(rows, "d", pairs)


def anchor_over_second(held):
    pieces = held[: 2 * PIECE]
    for a in range(1, 4):
        pairs = [(device(c, 0, 0, 0, 0), device(c, a, 0, 0, 0)) for c in range(NC)]
        pieces = pieces + send(held[2 * a * PIECE : 2 * (a + 1) * PIECE], pairs)
    pairs = [(device(c, a, 0, 0, 0), device(c, a, 0, 0, 1)) for c in range(NC) for a in range(4)]
    return pieces[:PIECE] + send(pieces[PIECE:], pairs)


def anchor_over_first(piece):
    lines = [(c, a, zl) for c in range(NC) for a in range(4) for zl in range(2)]
    steps = (
        [(device(c, a, 0, 0, zl), device(c, a, u, 0, zl)) for c, a, zl in lines]
        for u in range(1, 4)
    )
    piece = sum((send(piece, pairs) for pairs in steps), piece)
    steps = (
        [(device(c, a, u, 0, zl), device(c, a, u, zh, zl)) for c, a, zl in lines for u in range(4)]
        for zh in range(1, 4)
    )
    return sum((send(piece, pairs) for pairs in steps), piece)


def on_device(queries, keys, values, keep_index):
    me = lax.axis_index("d")
    block = me.astype(jnp.int32).reshape(1)
    swap = functools.partial(
        lax.ppermute, axis_name="d", perm=[(i, i ^ 1) for i in range(DEVICES)]
    )

    def gather(slots, groups):
        return lax.all_to_all(slots, "d", 0, 0, tiled=True, axis_index_groups=groups)

    given = (KEPT + HALF * 2 * TOK, HD)
    mine, sent = small_call(
        pick_kernel,
        (block, keep_index, jnp.concatenate([keys, values], axis=1)),
        [in_smem, in_smem, in_vmem],
        (given, given),
        4,
    )
    came = swap(sent)
    base = anchor_over_second(mine[KEPT:] + came[KEPT:])
    (slots,) = small_call(
        first_kernel,
        (block, mine, came),
        [in_smem, in_vmem, in_vmem],
        ((FIRST, KEPT_ROWS, HD),),
        4,
    )
    near = gather(slots, first_groups())
    (slots,) = small_call(second_kernel, (near, anchor_over_first(base)), [in_vmem, in_vmem], ((SECOND, SLOT, HD),), 8)
    far = gather(slots, second_groups())
    far_other = swap(far)

    out = attend(block, queries, keys, values, far, None, False)
    return attend(block, queries, keys, values, far_other, out, True)


def solution(mesh):
    line = Mesh(mesh.devices.reshape(DEVICES), ("d",))
    return jax.shard_map(
        on_device,
        mesh=line,
        in_specs=(P("d", None), P("d", None), P("d", None), P("d", None, None)),
        out_specs=P("d", None),
        check_vma=False,
    )
```

```python
import functools
import math

import jax
import jax.numpy as jnp
from jax import lax
from jax.experimental import pallas as pl
from jax.experimental.pallas import tpu as pltpu
from jax.sharding import Mesh, PartitionSpec as P

QH = 32
KVH = 4
HD = 128
KEEP = 8
TOK = 128
GROUP = QH // KVH
NX, NY, NZ, NC = 4, 4, 8, 2
DEVICES = NX * NY * NZ * NC
HALF = KVH // NC
FIRST = 16
SECOND = 8
PAIR = NC * KEEP
KEPT = HALF * PAIR
KEPT_ROWS = HALF * 2 * PAIR
CHUNK = FIRST * PAIR
PIECE = HALF * 2 * TOK // SECOND
SLOT = HALF * 2 * CHUNK + PIECE
PLANE = NY * NZ * NC * KEEP
PART = 4 * PAIR
EXP2_SCALE = math.log2(math.e) / math.sqrt(HD)
MIB = 1024 * 1024

bf16 = jnp.bfloat16
f32 = jnp.float32
in_smem = pl.BlockSpec(memory_space=pltpu.SMEM)
in_vmem = pl.BlockSpec(memory_space=pltpu.VMEM)


def at(x, y, z, core):
    return ((x * NY + y) * NZ + z) * NC + core


def device(core, a, u, zh, zl):
    x, y = (a, u) if core == 0 else (u, a)
    z = (2 * zh + zl) % NZ if core == 0 else (2 * zh - zl) % NZ
    return at(x, y, z, core)


def first_groups():
    return [
        [device(c, a, u, zh, zl) for u in range(4) for zh in range(4)]
        for c in range(2)
        for a in range(4)
        for zl in range(2)
    ]


def second_groups():
    return [
        [device(c, a, u, zh, zl) for a in range(4) for zl in range(2)]
        for c in range(2)
        for u in range(4)
        for zh in range(4)
    ]


def pick_kernel(block_ref, index_ref, both_ref, mine_ref, sent_ref):
    block = block_ref[0]
    core = block % NC
    rows = lax.broadcasted_iota(jnp.int32, (KEEP, TOK), 0)
    lanes = lax.broadcasted_iota(jnp.int32, (KEEP, TOK), 1)
    for out_ref, owner in ((sent_ref, 1 - core), (mine_ref, core)):
        for h in range(HALF):
            j = owner * HALF + h
            chosen = jnp.zeros((KEEP, TOK), jnp.int32)
            for r in range(KEEP):
                chosen = jnp.where(rows == r, index_ref[0, j, r], chosen)
            onehot = (chosen == lanes).astype(f32).astype(bf16)
            keys = both_ref[:, pl.ds(pl.multiple_of(j * HD, HD), HD)]
            values = both_ref[:, pl.ds(pl.multiple_of((KVH + j) * HD, HD), HD)]
            key_rows = jnp.dot(onehot, keys, preferred_element_type=f32)
            value_rows = jnp.dot(onehot, values, preferred_element_type=f32)
            found = jnp.concatenate([key_rows, value_rows], axis=0).astype(bf16)
            out_ref[h * PAIR : (h + 1) * PAIR] = found
            whole = jnp.concatenate([keys, values], axis=0)
            put = KEPT + 2 * h * TOK
            out_ref[put : put + 2 * TOK] = jnp.where(block == 0, whole, jnp.zeros_like(whole))


def first_kernel(block_ref, mine_ref, came_ref, out_ref):
    core = block_ref[0] % NC
    for h in range(HALF):
        mine = mine_ref[h * PAIR : (h + 1) * PAIR].astype(f32)
        came = came_ref[h * PAIR : (h + 1) * PAIR].astype(f32)
        low = jnp.where(core == 0, mine, came)
        high = jnp.where(core == 0, came, mine)
        keys = jnp.concatenate([low[:KEEP], high[:KEEP]], axis=0).astype(bf16)
        values = jnp.concatenate([low[KEEP:], high[KEEP:]], axis=0).astype(bf16)
        for k in range(FIRST):
            out_ref[k, 2 * h * PAIR : (2 * h + 1) * PAIR] = keys
            out_ref[k, (2 * h + 1) * PAIR : (2 * h + 2) * PAIR] = values


def second_kernel(in_ref, piece_ref, out_ref):
    for m in range(FIRST):
        for part in range(HALF * 2):
            rows = in_ref[m, part * PAIR : (part + 1) * PAIR]
            put = part * CHUNK + m * PAIR
            for s in range(SECOND):
                out_ref[s, put : put + PAIR] = rows
    for s in range(SECOND):
        out_ref[s, HALF * 2 * CHUNK :] = piece_ref[...]


def small_call(kernel, operands, in_specs, shapes, limit):
    return pl.pallas_call(
        kernel,
        in_specs=in_specs,
        out_specs=tuple(in_vmem for _ in shapes),
        out_shape=tuple(jax.ShapeDtypeStruct(s, bf16) for s in shapes),
        compiler_params=pltpu.CompilerParams(vmem_limit_bytes=limit * MIB),
    )(*operands)


def attend_kernel(other, block_ref, q_ref, k_ref, v_ref, far_ref, *refs):
    out_ref, key_rows, value_rows, even, odd, third = refs[-6:]
    block = block_ref[0]
    core = block % NC
    source = 1 - core if other else core
    first_head = source * HALF

    def columns_of(j, width):
        return pl.ds(pl.multiple_of(j * width, width), width)

    def run(full, planes):
        far = planes * PLANE
        keys = far + 2 * TOK

        def put(h, start, count, new_keys, new_values, valid):
            if valid is None:
                key_rows[h, start : start + count, :] = new_keys
                value_rows[h, start : start + count, :HD] = new_values
                value_rows[h, start : start + count, HD:] = jnp.ones((count, HD), bf16)
            else:
                first_key = k_ref[0:1, columns_of(first_head + h, HD)]
                spare = jnp.ones((count, HD), bf16) - valid
                key_rows[h, start : start + count, :] = new_keys * valid + first_key * spare
                value_rows[h, start : start + count, :HD] = new_values * valid
                value_rows[h, start : start + count, HD:] = valid

        def gather_rows(h):
            rows = lax.broadcasted_iota(jnp.int32, (PART, HD), 0)
            zh, half = rows // PAIR, (rows // KEEP) % NC
            for x in range(planes):
                for i in range(PLANE // PART):
                    slot = jnp.where(source == 0, 2 * x + i // 4, i)
                    row = jnp.where(source == 0, (i % 4) * PART, x * PART) + h * 2 * CHUNK
                    row = pl.multiple_of(row, PART)
                    valid = None
                    if x >= full or (x == 0 and i == 0):
                        y = jnp.where(source == 0, i % 4, i // 2)
                        shift = jnp.where(source == 0, i // 4, NZ - i % 2)
                        owner = at(x, y, (2 * zh + shift) % NZ, half)
                        valid = ((owner >= 1) & (owner < block)).astype(f32).astype(bf16)
                    put(
                        h,
                        x * PLANE + i * PART,
                        PART,
                        far_ref[slot, pl.ds(row, PART), :],
                        far_ref[slot, pl.ds(pl.multiple_of(row + CHUNK, PART), PART), :],
                        valid,
                    )
            j = first_head + h
            valid = None
            if full == 0:
                valid = jnp.where(block > 0, jnp.ones((PIECE, HD), f32), 0.0).astype(bf16)
            for i in range(TOK // PIECE):
                put(
                    h,
                    far + i * PIECE,
                    PIECE,
                    far_ref[h * 4 + i, HALF * 2 * CHUNK :, :],
                    far_ref[h * 4 + 2 + i, HALF * 2 * CHUNK :, :],
                    valid,
                )
            put(
                h,
                far + TOK,
                TOK,
                k_ref[:, columns_of(j, HD)],
                v_ref[:, columns_of(j, HD)],
                None,
            )

        causal = lax.broadcasted_iota(jnp.int32, (TOK, TOK), 1) <= lax.broadcasted_iota(
            jnp.int32, (TOK, TOK), 0
        )

        def scores(unit, held):
            found = lax.dot_general(
                q_ref[:, columns_of(first_head * GROUP + unit, HD)],
                key_rows[unit // GROUP, :keys, :],
                (((1,), (1,)), ((), ())),
                preferred_element_type=f32,
            )
            held[:, : keys - TOK] = found[:, : keys - TOK]
            held[:, keys - TOK : keys] = jnp.where(causal, found[:, keys - TOK :], -1e30)

        def finish(unit, held):
            found = held[:, :keys]
            highest = jnp.max(found, axis=1, keepdims=True)
            weights = jnp.exp2((found - highest) * EXP2_SCALE).astype(bf16)
            summed = jnp.dot(
                weights, value_rows[unit // GROUP, :keys, :], preferred_element_type=f32
            )
            out_ref[:, columns_of(unit, HD)] = (summed[:, :HD] / summed[:, HD:]).astype(bf16)

        units = HALF * GROUP
        gather_rows(0)
        buffers = (even, odd, third)
        scores(0, even)
        scores(1, odd)
        for unit in range(units):
            if unit == GROUP // 2:
                gather_rows(1)
            if unit + 2 < units:
                scores(unit + 2, buffers[(unit + 2) % 3])
            finish(unit, buffers[unit % 3])

    own_plane = block // (NY * NZ * NC)
    for low, high in ((0, 1), (1, 2), (2, 3), (3, 4)):
        here = (own_plane >= low) & (own_plane < high)
        pl.when(here)(functools.partial(run, low, high))


def attend(block, queries, keys, values, far, out, other):
    def half(i, block_ref):
        core = block_ref[0] % NC
        return (0, 1 - core if other else core)

    operands = [queries, keys, values, far]
    in_specs = [in_vmem] * len(operands)
    aliases = {}
    if out is not None:
        operands.append(out)
        in_specs.append(pl.BlockSpec(memory_space=pl.ANY))
        aliases = {len(operands): 0}
    rows = NX * PLANE + 2 * TOK
    work = HALF * GROUP * TOK * rows
    return pl.pallas_call(
        functools.partial(attend_kernel, other),
        grid_spec=pltpu.PrefetchScalarGridSpec(
            num_scalar_prefetch=1,
            grid=(1,),
            in_specs=in_specs,
            out_specs=pl.BlockSpec((TOK, HALF * GROUP * HD), half),
            scratch_shapes=[
                pltpu.VMEM((HALF, rows, HD), bf16),
                pltpu.VMEM((HALF, rows, 2 * HD), bf16),
                pltpu.VMEM((TOK, rows), f32),
                pltpu.VMEM((TOK, rows), f32),
                pltpu.VMEM((TOK, rows), f32),
            ],
        ),
        out_shape=jax.ShapeDtypeStruct((TOK, QH * HD), bf16),
        input_output_aliases=aliases,
        compiler_params=pltpu.CompilerParams(vmem_limit_bytes=32 * MIB),
        cost_estimate=pl.CostEstimate(
            flops=4 * work * HD, bytes_accessed=4 * MIB, transcendentals=work
        ),
    )(block, *operands)


def send(rows, pairs):
    return lax.ppermute(rows, "d", pairs)


def anchor_over_second(held):
    pieces = held[: 2 * PIECE]
    for a in (1, 3, 2):
        pairs = [(device(c, 0, 0, 0, 0), device(c, a, 0, 0, 0)) for c in range(NC)]
        pieces = pieces + send(held[2 * a * PIECE : 2 * (a + 1) * PIECE], pairs)
    pairs = [(device(c, a, 0, 0, 0), device(c, a, 0, 0, 1)) for c in range(NC) for a in range(4)]
    return pieces[:PIECE] + send(pieces[PIECE:], pairs)


def anchor_over_first(piece):
    lines = [(c, a, zl) for c in range(NC) for a in range(4) for zl in range(2)]
    steps = (
        [(device(c, a, 0, 0, zl), device(c, a, u, 0, zl)) for c, a, zl in lines]
        for u in (1, 3, 2)
    )
    piece = sum((send(piece, pairs) for pairs in steps), piece)
    steps = (
        [(device(c, a, u, 0, zl), device(c, a, u, zh, zl)) for c, a, zl in lines for u in range(4)]
        for zh in range(1, 4)
    )
    return sum((send(piece, pairs) for pairs in steps), piece)


def on_device(queries, keys, values, keep_index):
    me = lax.axis_index("d")
    block = me.astype(jnp.int32).reshape(1)
    swap = functools.partial(
        lax.ppermute, axis_name="d", perm=[(i, i ^ 1) for i in range(DEVICES)]
    )

    def gather(slots, groups):
        return lax.all_to_all(slots, "d", 0, 0, tiled=True, axis_index_groups=groups)

    given = (KEPT + HALF * 2 * TOK, HD)
    mine, sent = small_call(
        pick_kernel,
        (block, keep_index, jnp.concatenate([keys, values], axis=1)),
        [in_smem, in_smem, in_vmem],
        (given, given),
        4,
    )
    came = swap(sent)
    base = anchor_over_second(mine[KEPT:] + came[KEPT:])
    (slots,) = small_call(
        first_kernel,
        (block, mine, came),
        [in_smem, in_vmem, in_vmem],
        ((FIRST, KEPT_ROWS, HD),),
        4,
    )
    near = gather(slots, first_groups())
    (slots,) = small_call(second_kernel, (near, anchor_over_first(base)), [in_vmem, in_vmem], ((SECOND, SLOT, HD),), 8)
    far = gather(slots, second_groups())
    far_other = swap(far)

    out = attend(block, queries, keys, values, far, None, False)
    return attend(block, queries, keys, values, far_other, out, True)


def solution(mesh):
    line = Mesh(mesh.devices.reshape(DEVICES), ("d",))
    return jax.shard_map(
        on_device,
        mesh=line,
        in_specs=(P("d", None), P("d", None), P("d", None), P("d", None, None)),
        out_specs=P("d", None),
        check_vma=False,
    )
```

```python
import functools
import math

import jax
import jax.numpy as jnp
from jax import lax
from jax.experimental import pallas as pl
from jax.experimental.pallas import tpu as pltpu
from jax.sharding import Mesh, PartitionSpec as P

QH = 32
KVH = 4
HD = 128
KEEP = 8
TOK = 128
GROUP = QH // KVH
NX, NY, NZ, NC = 4, 4, 8, 2
DEVICES = NX * NY * NZ * NC
HALF = KVH // NC
FIRST = 16
SECOND = 8
PAIR = NC * KEEP
KEPT = HALF * PAIR
KEPT_ROWS = HALF * 2 * PAIR
CHUNK = FIRST * PAIR
PIECE = HALF * 2 * TOK // SECOND
SLOT = HALF * 2 * CHUNK + PIECE
PLANE = NY * NZ * NC * KEEP
PART = 4 * PAIR
EXP2_SCALE = math.log2(math.e) / math.sqrt(HD)
MIB = 1024 * 1024

bf16 = jnp.bfloat16
f32 = jnp.float32
in_smem = pl.BlockSpec(memory_space=pltpu.SMEM)
in_vmem = pl.BlockSpec(memory_space=pltpu.VMEM)


def at(x, y, z, core):
    return ((x * NY + y) * NZ + z) * NC + core


def device(core, a, u, zh, zl):
    x, y = (a, u) if core == 0 else (u, a)
    z = (2 * zh + zl) % NZ if core == 0 else (2 * zh - zl) % NZ
    return at(x, y, z, core)


def first_groups():
    return [
        [device(c, a, u, zh, zl) for u in range(4) for zh in range(4)]
        for c in range(2)
        for a in range(4)
        for zl in range(2)
    ]


def second_groups():
    return [
        [device(c, a, u, zh, zl) for a in range(4) for zl in range(2)]
        for c in range(2)
        for u in range(4)
        for zh in range(4)
    ]


def pick_kernel(block_ref, index_ref, both_ref, mine_ref, sent_ref):
    block = block_ref[0]
    core = block % NC
    rows = lax.broadcasted_iota(jnp.int32, (KEEP, TOK), 0)
    lanes = lax.broadcasted_iota(jnp.int32, (KEEP, TOK), 1)
    for out_ref, owner in ((sent_ref, 1 - core), (mine_ref, core)):
        for h in range(HALF):
            j = owner * HALF + h
            chosen = jnp.zeros((KEEP, TOK), jnp.int32)
            for r in range(KEEP):
                chosen = jnp.where(rows == r, index_ref[0, j, r], chosen)
            onehot = (chosen == lanes).astype(f32).astype(bf16)
            keys = both_ref[:, pl.ds(pl.multiple_of(j * HD, HD), HD)]
            values = both_ref[:, pl.ds(pl.multiple_of((KVH + j) * HD, HD), HD)]
            key_rows = jnp.dot(onehot, keys, preferred_element_type=f32)
            value_rows = jnp.dot(onehot, values, preferred_element_type=f32)
            found = jnp.concatenate([key_rows, value_rows], axis=0).astype(bf16)
            out_ref[h * PAIR : (h + 1) * PAIR] = found
            whole = jnp.concatenate([keys, values], axis=0)
            put = KEPT + 2 * h * TOK
            out_ref[put : put + 2 * TOK] = jnp.where(block == 0, whole, jnp.zeros_like(whole))


def first_kernel(block_ref, mine_ref, came_ref, out_ref):
    core = block_ref[0] % NC
    for h in range(HALF):
        mine = mine_ref[h * PAIR : (h + 1) * PAIR].astype(f32)
        came = came_ref[h * PAIR : (h + 1) * PAIR].astype(f32)
        low = jnp.where(core == 0, mine, came)
        high = jnp.where(core == 0, came, mine)
        keys = jnp.concatenate([low[:KEEP], high[:KEEP]], axis=0).astype(bf16)
        values = jnp.concatenate([low[KEEP:], high[KEEP:]], axis=0).astype(bf16)
        for k in range(FIRST):
            out_ref[k, 2 * h * PAIR : (2 * h + 1) * PAIR] = keys
            out_ref[k, (2 * h + 1) * PAIR : (2 * h + 2) * PAIR] = values


def second_kernel(in_ref, piece_ref, out_ref):
    for m in range(FIRST):
        for part in range(HALF * 2):
            rows = in_ref[m, part * PAIR : (part + 1) * PAIR]
            put = part * CHUNK + m * PAIR
            for s in range(SECOND):
                out_ref[s, put : put + PAIR] = rows
    for s in range(SECOND):
        out_ref[s, HALF * 2 * CHUNK :] = piece_ref[...]


def small_call(kernel, operands, in_specs, shapes, limit):
    return pl.pallas_call(
        kernel,
        in_specs=in_specs,
        out_specs=tuple(in_vmem for _ in shapes),
        out_shape=tuple(jax.ShapeDtypeStruct(s, bf16) for s in shapes),
        compiler_params=pltpu.CompilerParams(vmem_limit_bytes=limit * MIB),
    )(*operands)


def attend_kernel(other, block_ref, q_ref, k_ref, v_ref, far_ref, *refs):
    out_ref, key_rows, value_rows, even, odd, third = refs[-6:]
    block = block_ref[0]
    core = block % NC
    source = 1 - core if other else core
    first_head = source * HALF

    def columns_of(j, width):
        return pl.ds(pl.multiple_of(j * width, width), width)

    def run(full, planes):
        far = planes * PLANE
        keys = far + 2 * TOK

        def put(h, start, count, new_keys, new_values, valid):
            if valid is None:
                key_rows[h, start : start + count, :] = new_keys
                value_rows[h, start : start + count, :HD] = new_values
                value_rows[h, start : start + count, HD:] = jnp.ones((count, HD), bf16)
            else:
                first_key = k_ref[0:1, columns_of(first_head + h, HD)]
                spare = jnp.ones((count, HD), bf16) - valid
                key_rows[h, start : start + count, :] = new_keys * valid + first_key * spare
                value_rows[h, start : start + count, :HD] = new_values * valid
                value_rows[h, start : start + count, HD:] = valid

        def gather_rows(h):
            rows = lax.broadcasted_iota(jnp.int32, (PART, HD), 0)
            zh, half = rows // PAIR, (rows // KEEP) % NC
            for x in range(planes):
                for i in range(PLANE // PART):
                    slot = jnp.where(source == 0, 2 * x + i // 4, i)
                    row = jnp.where(source == 0, (i % 4) * PART, x * PART) + h * 2 * CHUNK
                    row = pl.multiple_of(row, PART)
                    valid = None
                    if x >= full or (x == 0 and i == 0):
                        y = jnp.where(source == 0, i % 4, i // 2)
                        shift = jnp.where(source == 0, i // 4, NZ - i % 2)
                        owner = at(x, y, (2 * zh + shift) % NZ, half)
                        valid = ((owner >= 1) & (owner < block)).astype(f32).astype(bf16)
                    put(
                        h,
                        x * PLANE + i * PART,
                        PART,
                        far_ref[slot, pl.ds(row, PART), :],
                        far_ref[slot, pl.ds(pl.multiple_of(row + CHUNK, PART), PART), :],
                        valid,
                    )
            j = first_head + h
            valid = None
            if full == 0:
                valid = jnp.where(block > 0, jnp.ones((PIECE, HD), f32), 0.0).astype(bf16)
            for i in range(TOK // PIECE):
                put(
                    h,
                    far + i * PIECE,
                    PIECE,
                    far_ref[h * 4 + i, HALF * 2 * CHUNK :, :],
                    far_ref[h * 4 + 2 + i, HALF * 2 * CHUNK :, :],
                    valid,
                )
            put(
                h,
                far + TOK,
                TOK,
                k_ref[:, columns_of(j, HD)],
                v_ref[:, columns_of(j, HD)],
                None,
            )

        causal = lax.broadcasted_iota(jnp.int32, (TOK, TOK), 1) <= lax.broadcasted_iota(
            jnp.int32, (TOK, TOK), 0
        )

        def scores(unit, held):
            found = lax.dot_general(
                q_ref[:, columns_of(first_head * GROUP + unit, HD)],
                key_rows[unit // GROUP, :keys, :],
                (((1,), (1,)), ((), ())),
                preferred_element_type=f32,
            )
            held[:, : keys - TOK] = found[:, : keys - TOK]
            held[:, keys - TOK : keys] = jnp.where(causal, found[:, keys - TOK :], -1e30)

        def finish(unit, held):
            found = held[:, :keys]
            highest = jnp.max(found, axis=1, keepdims=True)
            weights = jnp.exp2((found - highest) * EXP2_SCALE).astype(bf16)
            summed = jnp.dot(
                weights, value_rows[unit // GROUP, :keys, :], preferred_element_type=f32
            )
            out_ref[:, columns_of(unit, HD)] = (summed[:, :HD] / summed[:, HD:]).astype(bf16)

        units = HALF * GROUP
        gather_rows(0)
        buffers = (even, odd, third)
        scores(0, even)
        scores(1, odd)
        for unit in range(units):
            if unit == GROUP // 2:
                gather_rows(1)
            if unit + 2 < units:
                scores(unit + 2, buffers[(unit + 2) % 3])
            finish(unit, buffers[unit % 3])

    own_plane = block // (NY * NZ * NC)
    for low, high in ((0, 1), (1, 2), (2, 3), (3, 4)):
        here = (own_plane >= low) & (own_plane < high)
        pl.when(here)(functools.partial(run, low, high))


def attend(block, queries, keys, values, far, out, other):
    def half(i, block_ref):
        core = block_ref[0] % NC
        return (0, 1 - core if other else core)

    operands = [queries, keys, values, far]
    in_specs = [in_vmem] * len(operands)
    aliases = {}
    if out is not None:
        operands.append(out)
        in_specs.append(pl.BlockSpec(memory_space=pl.ANY))
        aliases = {len(operands): 0}
    rows = NX * PLANE + 2 * TOK
    work = HALF * GROUP * TOK * rows
    return pl.pallas_call(
        functools.partial(attend_kernel, other),
        grid_spec=pltpu.PrefetchScalarGridSpec(
            num_scalar_prefetch=1,
            grid=(1,),
            in_specs=in_specs,
            out_specs=pl.BlockSpec((TOK, HALF * GROUP * HD), half),
            scratch_shapes=[
                pltpu.VMEM((HALF, rows, HD), bf16),
                pltpu.VMEM((HALF, rows, 2 * HD), bf16),
                pltpu.VMEM((TOK, rows), f32),
                pltpu.VMEM((TOK, rows), f32),
                pltpu.VMEM((TOK, rows), f32),
            ],
        ),
        out_shape=jax.ShapeDtypeStruct((TOK, QH * HD), bf16),
        input_output_aliases=aliases,
        compiler_params=pltpu.CompilerParams(vmem_limit_bytes=32 * MIB),
        cost_estimate=pl.CostEstimate(
            flops=4 * work * HD, bytes_accessed=4 * MIB, transcendentals=work
        ),
    )(block, *operands)


def send(rows, pairs):
    return lax.ppermute(rows, "d", pairs)


def anchor_over_second(held):
    pieces = held[: 2 * PIECE]
    for a in (1, 3, 2):
        pairs = [(device(c, 0, 0, 0, 0), device(c, a, 0, 0, 0)) for c in range(NC)]
        pieces = pieces + send(held[2 * a * PIECE : 2 * (a + 1) * PIECE], pairs)
    pairs = [(device(c, a, 0, 0, 0), device(c, a, 0, 0, 1)) for c in range(NC) for a in range(4)]
    return pieces[:PIECE] + send(pieces[PIECE:], pairs)


def anchor_over_first(piece):
    lines = [(c, a, zl) for c in range(NC) for a in range(4) for zl in range(2)]
    steps = (
        [(device(c, a, 0, 0, zl), device(c, a, u, 0, zl)) for c, a, zl in lines]
        for u in (1, 3, 2)
    )
    piece = sum((send(piece, pairs) for pairs in steps), piece)
    steps = (
        [(device(c, a, u, 0, zl), device(c, a, u, zh, zl)) for c, a, zl in lines for u in range(4)]
        for zh in (1, 3, 2)
    )
    return sum((send(piece, pairs) for pairs in steps), piece)


def on_device(queries, keys, values, keep_index):
    me = lax.axis_index("d")
    block = me.astype(jnp.int32).reshape(1)
    swap = functools.partial(
        lax.ppermute, axis_name="d", perm=[(i, i ^ 1) for i in range(DEVICES)]
    )

    def gather(slots, groups):
        return lax.all_to_all(slots, "d", 0, 0, tiled=True, axis_index_groups=groups)

    given = (KEPT + HALF * 2 * TOK, HD)
    mine, sent = small_call(
        pick_kernel,
        (block, keep_index, jnp.concatenate([keys, values], axis=1)),
        [in_smem, in_smem, in_vmem],
        (given, given),
        4,
    )
    came = swap(sent)
    base = anchor_over_second(mine[KEPT:] + came[KEPT:])
    (slots,) = small_call(
        first_kernel,
        (block, mine, came),
        [in_smem, in_vmem, in_vmem],
        ((FIRST, KEPT_ROWS, HD),),
        4,
    )
    near = gather(slots, first_groups())
    (slots,) = small_call(second_kernel, (near, anchor_over_first(base)), [in_vmem, in_vmem], ((SECOND, SLOT, HD),), 8)
    far = gather(slots, second_groups())
    far_other = swap(far)

    out = attend(block, queries, keys, values, far, None, False)
    return attend(block, queries, keys, values, far_other, out, True)


def solution(mesh):
    line = Mesh(mesh.devices.reshape(DEVICES), ("d",))
    return jax.shard_map(
        on_device,
        mesh=line,
        in_specs=(P("d", None), P("d", None), P("d", None), P("d", None, None)),
        out_specs=P("d", None),
        check_vma=False,
    )
```
